32 devices in a mesh: groups: 2 (over y), fsdp: 4 (over z), sub: 2 (over x), rep: 2 (over core).
Axes of the slice: x: 2, y: 2, z: 4, core: 2. Of those that a mesh axis runs over, the one named last changes fastest.
Arguments:
- activations: bfloat16 [6144, 8192], P(('groups', 'fsdp', 'rep'), 'sub'), parts along dimension 0, may hold values from -6 to 6
- cotangent: bfloat16 [6144, 1024], P(('groups', 'fsdp', 'rep'), 'sub'), parts along dimension 0, may hold values from -6 to 6
- base_weight: bfloat16 [1024, 8192], P('fsdp', 'sub'), may hold values from -0.0625 to 0.0625
- adapter_down: bfloat16 [16, 8192, 64], P(('groups', 'fsdp'), 'sub'), parts along dimension 0, may hold values from -0.0625 to 0.0625
- adapter_up: bfloat16 [16, 64, 1024], P(('groups', 'fsdp'), None, 'sub'), parts along dimension 0, may hold values from -0.75 to 0.75
- tile_counts: int32 [16], P('groups'), parts along dimension 0, may hold values from 1 to 3, as said below
- tile_length: int32 [48], P(('groups', 'fsdp', 'rep')), parts along dimension 0, may hold values from 1 to 128
- tile_adapter: int32 [48], P(('groups', 'fsdp', 'rep')), parts along dimension 0, may hold values from 0 to 1
Outputs:
- value_proj: bfloat16 [6144, 1024], P(('groups', 'fsdp', 'rep'), 'sub'), parts along dimension 0
- input_grad: bfloat16 [6144, 8192], P(('groups', 'fsdp', 'rep'), 'sub'), parts along dimension 0
- down_grad: bfloat16 [16, 8192, 64], P(('groups', 'fsdp'), 'sub'), parts along dimension 0
- up_grad: bfloat16 [16, 64, 1024], P(('groups', 'fsdp'), None, 'sub'), parts along dimension 0
The draws below stay inside these ranges and needn't reach their ends.
There are 2 independent parts, one for each index of `groups`. The reference program is written for one: setup_inputs(seed, part) draws one part's arguments, and reference() takes and returns one part's arrays. A program takes and returns all parts, laid end to end along the dimension named above; an argument that names none is the same for every part. Nothing has to cross between parts.
Inputs may be any that keep to these rules, and one draw needn't show every extreme that they name: tile_counts[f * 2 + r] is the number of leading slots in use at fsdp index f and rep index r; the two counts of one fsdp index add up to at most 4, and 3 occurs in every draw.
All inputs are finite; a program needn't handle non-finite values.
Results may differ from the reference program's by a relative error of at most 0.0049.
Values may be sent and summed in bfloat16 or wider, within the bound.
A program may use at most 64 MiB of HBM per device.

```python
import jax
import jax.numpy as jnp
from jax import lax

MODEL_WIDTH = 8192
VALUE_WIDTH = 1024
R = 64
TILE_TOKENS = 128
SLOTS = 3
A_DEV = 2
NA = 8
DEVS = 8
ROWS = 3072
N_FSDP = 4
N_REP = 2


def draw_tile_counts(key, part):
    key = jax.random.fold_in(key, 11)
    pattern = jax.random.randint(key, (N_FSDP,), 0, 6)
    pattern = pattern.at[0].set(0)
    first_table = jnp.array([3, 1, 2, 2, 1, 1], dtype=jnp.int32)
    second_table = jnp.array([1, 3, 2, 1, 2, 1], dtype=jnp.int32)
    first_half = first_table[pattern]
    second_half = second_table[pattern]
    return jnp.stack([first_half, second_half], 1).reshape(-1).astype(jnp.int32)


def set_ends(drawn, stream_key, low, top_value):
    shape = drawn.shape
    place = [jax.random.randint(jax.random.fold_in(stream_key, axis), (), 0, shape[axis]) for axis in range(len(shape))]
    drawn = drawn.at[tuple(place)].set(low)
    longest = shape.index(max(shape))
    place[longest] = (place[longest] + 1) % shape[longest]
    return drawn.at[tuple(place)].set(top_value)


def shard_levels(key, dims, shards, smallest, high):
    factor_of, own = 1.0, jax.random.fold_in(key, 6)
    for dim, parts in shards:
        steps = jnp.exp(jax.random.uniform(jax.random.fold_in(own, dim), (parts,), jnp.float32, smallest / len(shards), high / len(shards)))
        factor_of = factor_of * jnp.repeat(steps, dims[dim] // parts).reshape([-1 if axis == dim else 1 for axis in range(len(dims))])
    return factor_of


def bell_draw(own_key, shape, spread, bound, cuts=(), kind=jnp.bfloat16):
    values = jax.random.normal(own_key, shape, jnp.float32) * spread
    if len(cuts) > 0:
        values = shard_levels(own_key, shape, cuts, -0.22, 0.18) * values
    return jnp.clip(values, min=-bound, max=bound).astype(kind)


def setup_inputs(seed: int = 0, part: int = 0) -> dict:
    key_of = jax.random.split(jax.random.key(seed), 9)
    own_keys = jax.random.split(jax.random.fold_in(key_of[8], part), 9)
    activations = bell_draw(own_keys[0], (ROWS, MODEL_WIDTH), 1.0, 6.0, ((0, 8), (1, 2)))
    cotangent = bell_draw(own_keys[1], (ROWS, VALUE_WIDTH), 1.0, 6.0, ((0, 8), (1, 2)))
    base_weight = bell_draw(key_of[2], (VALUE_WIDTH, MODEL_WIDTH), MODEL_WIDTH ** -0.5, 0.0625, ((0, 4), (1, 2)))
    adapter_down = bell_draw(own_keys[3], (NA, MODEL_WIDTH, R), MODEL_WIDTH ** -0.5, 0.0625, ((0, 4), (1, 2)))
    adapter_up = bell_draw(own_keys[4], (NA, R, VALUE_WIDTH), R ** -0.5, 0.75, ((0, 4), (2, 2)))
    tile_counts = draw_tile_counts(jax.random.fold_in(jax.random.fold_in(key_of[8], part), 71), part)
    tile_length = set_ends(jax.random.randint(own_keys[6], (DEVS * SLOTS,), 1, TILE_TOKENS + 1), jax.random.fold_in(own_keys[6], 1), 1, TILE_TOKENS).astype(jnp.int32)
    tile_adapter = set_ends(jax.random.randint(own_keys[7], (DEVS * SLOTS,), 0, A_DEV), jax.random.fold_in(own_keys[7], 1), 0, A_DEV - 1).astype(jnp.int32)
    return dict(activations=activations, cotangent=cotangent, base_weight=base_weight, adapter_down=adapter_down, adapter_up=adapter_up, tile_counts=tile_counts, tile_length=tile_length, tile_adapter=tile_adapter)


adapter_scale = 2.0


def reference(activations, cotangent, base_weight, adapter_down, adapter_up, tile_counts, tile_length, tile_adapter):
    tile_grand_sum = tile_length.shape[0]
    tile_index = jnp.arange(tile_grand_sum, dtype=jnp.int32)
    device_row = (tile_index // SLOTS).astype(jnp.int32)
    slot_index = tile_index % SLOTS
    in_use = slot_index < tile_counts[device_row]
    positions = jnp.arange(TILE_TOKENS, dtype=jnp.int32)
    row_valid = (in_use[:, None] & (positions[None, :] < tile_length[:, None])).astype(jnp.bfloat16)
    global_adapter = ((device_row // N_REP) * A_DEV + tile_adapter).astype(jnp.int32)
    tokens = activations.reshape(tile_grand_sum, TILE_TOKENS, MODEL_WIDTH)
    masked_dy = cotangent.reshape(tile_grand_sum, TILE_TOKENS, VALUE_WIDTH) * row_valid[:, :, None]
    flat_dy = masked_dy.reshape(-1, VALUE_WIDTH)
    frozen_value_out = jnp.dot(activations, base_weight.T, preferred_element_type=jnp.float32)
    frozen_input_grad = jnp.dot(flat_dy, base_weight, preferred_element_type=jnp.float32)

    def per_tile(inputs):
        tile_token_rows, tile_output_grad, which = inputs
        down_factor = adapter_down[which]
        up_factor = adapter_up[which]
        low_in = jnp.dot(tile_token_rows, down_factor, preferred_element_type=jnp.float32).astype(jnp.bfloat16)
        low_grad = jnp.dot(tile_output_grad, up_factor.T, preferred_element_type=jnp.float32).astype(jnp.bfloat16)
        value_adapter_out = jnp.dot(low_in, up_factor, preferred_element_type=jnp.float32)
        input_adapter_grad = jnp.dot(low_grad, down_factor.T, preferred_element_type=jnp.float32)
        return low_in, low_grad, value_adapter_out, input_adapter_grad

    low_in, low_grad, value_adapter_out, input_adapter_grad = lax.map(per_tile, (tokens, masked_dy, global_adapter))
    value_total_out = frozen_value_out.reshape(tile_grand_sum, TILE_TOKENS, VALUE_WIDTH) + adapter_scale * value_adapter_out
    value_proj = (value_total_out * row_valid[:, :, None].astype(jnp.float32)).astype(jnp.bfloat16).reshape(-1, VALUE_WIDTH)
    input_total_grad = frozen_input_grad.reshape(tile_grand_sum, TILE_TOKENS, MODEL_WIDTH) + adapter_scale * input_adapter_grad
    input_grad = input_total_grad.astype(jnp.bfloat16).reshape(-1, MODEL_WIDTH)

    def accumulate(carry, inputs):
        down_sum, up_sum = carry
        tile_token_rows, tile_output_grad, tile_rank_input, tile_rank_grad, which = inputs
        down_product = adapter_scale * jnp.dot(tile_token_rows.T, tile_rank_grad, preferred_element_type=jnp.float32)
        up_product = adapter_scale * jnp.dot(tile_rank_input.T, tile_output_grad, preferred_element_type=jnp.float32)
        return (down_sum.at[which].add(down_product), up_sum.at[which].add(up_product)), None

    initial = (jnp.zeros(adapter_down.shape, jnp.float32), jnp.zeros(adapter_up.shape, jnp.float32))
    totals, unused = lax.scan(accumulate, initial, (tokens, masked_dy, low_in, low_grad, global_adapter))
    return value_proj, input_grad, totals[0].astype(jnp.bfloat16), totals[1].astype(jnp.bfloat16)
```

```python
import functools

import jax
import jax.numpy as jnp
from jax import lax
from jax.experimental import pallas as pl
from jax.experimental.pallas import tpu as pltpu
from jax.sharding import PartitionSpec as P

adapter_scale = 2.0


def on_device_general(
    activations,
    cotangent,
    base_weight,
    adapter_down,
    adapter_up,
    tile_counts,
    tile_length,
    tile_adapter,
):
    slot_count = tile_length.shape[0]
    tile_rows = activations.shape[0] // slot_count
    feat_width = activations.shape[1]
    head_width = cotangent.shape[1]
    own_sets = adapter_down.shape[0]
    low_rank = adapter_down.shape[2]
    rep_count = lax.axis_size("rep")
    fsdp_pos = lax.axis_index("fsdp")
    rep_pos = lax.axis_index("rep")
    own_count = tile_counts[fsdp_pos * rep_count + rep_pos]
    slot_ids = jnp.arange(slot_count, dtype=jnp.int32)
    positions = jnp.arange(tile_rows, dtype=jnp.int32)
    row_valid = (
        (slot_ids < own_count)[:, None] & (positions[None, :] < tile_length[:, None])
    ).astype(jnp.bfloat16)
    masked_dy = cotangent.reshape(slot_count, tile_rows, head_width) * row_valid[:, :, None]
    adapter_pick = (tile_adapter[:, None] == jnp.arange(own_sets, dtype=jnp.int32)[None, :]).astype(
        jnp.bfloat16
    )
    contract_last = (((1,), (1,)), ((), ()))
    contract_first = (((0,), (0,)), ((), ()))
    valid_rows = row_valid.reshape(-1)[:, None].astype(jnp.float32)
    work_dy = masked_dy.reshape(-1, head_width)
    row_count = activations.shape[0]
    set_count = adapter_down.shape[0]
    chosen_rows = jnp.broadcast_to(
        adapter_pick[:, None, :], (adapter_pick.shape[0], tile_rows, set_count)
    ).reshape(row_count, set_count)
    flattened_down = adapter_down.transpose(1, 0, 2).reshape(feat_width, set_count * low_rank)
    flat_up = adapter_up.reshape(set_count * low_rank, head_width)
    pick_adapter_rows = chosen_rows.astype(jnp.float32)[:, :, None]
    adapter_input_grad = jnp.dot(
        activations, flattened_down, preferred_element_type=jnp.float32
    ).reshape(row_count, set_count, low_rank)
    adapter_backward = lax.dot_general(
        work_dy, flat_up, contract_last, preferred_element_type=jnp.float32
    ).reshape(row_count, set_count, low_rank)
    input_piece = jnp.sum(adapter_input_grad * pick_adapter_rows, axis=1)
    backward_piece = jnp.sum(adapter_backward * pick_adapter_rows, axis=1)
    in_sum, back_sum = lax.psum((input_piece, backward_piece), "sub")
    in_low = in_sum.astype(jnp.bfloat16)
    back_low = back_sum.astype(jnp.bfloat16)
    in_wide = (chosen_rows[:, :, None] * in_low[:, None, :]).reshape(
        row_count, set_count * low_rank
    )
    back_wide = (chosen_rows[:, :, None] * back_low[:, None, :]).reshape(
        row_count, set_count * low_rank
    )
    full_dy = lax.all_gather(work_dy, "sub", axis=1, tiled=True)
    whole_weight = lax.all_gather(base_weight, "fsdp", axis=0, tiled=True)
    value_part = lax.dot_general(
        activations, whole_weight, contract_last, preferred_element_type=jnp.float32
    )
    input_frozen_grad = jnp.dot(full_dy, whole_weight, preferred_element_type=jnp.float32)
    value_frozen_out = lax.psum_scatter(value_part, "sub", scatter_dimension=1, tiled=True)
    value_total_out = value_frozen_out + adapter_scale * jnp.dot(
        in_wide, flat_up, preferred_element_type=jnp.float32
    )
    input_total_grad = input_frozen_grad + adapter_scale * lax.dot_general(
        back_wide, flattened_down, contract_last, preferred_element_type=jnp.float32
    )
    down_product = adapter_scale * lax.dot_general(
        activations, back_wide, contract_first, preferred_element_type=jnp.float32
    )
    up_product = adapter_scale * lax.dot_general(
        in_wide, work_dy, contract_first, preferred_element_type=jnp.float32
    )
    down_product = down_product.reshape(feat_width, set_count, low_rank).transpose(1, 0, 2)
    up_product = up_product.reshape(set_count, low_rank, head_width)
    value_total_out, input_total_grad, down_grad, up_grad = (
        value_total_out,
        input_total_grad,
        down_product,
        up_product,
    )
    down_total, up_total = lax.psum((down_grad, up_grad), "rep")
    value_proj = (value_total_out * valid_rows).astype(jnp.bfloat16)
    return (
        value_proj,
        input_total_grad.astype(jnp.bfloat16),
        down_total.astype(jnp.bfloat16),
        up_total.astype(jnp.bfloat16),
    )


CHUNKS = 4
NT = (((1,), (1,)), ((), ()))


def dot_nt(a, b):
    return lax.dot_general(a, b, NT, preferred_element_type=jnp.float32)


def dot_nn(a, b):
    return jnp.dot(a, b, preferred_element_type=jnp.float32)


def fused_kernel(
    counts,
    lengths,
    picks,
    act_h,
    dy_h,
    w_h,
    down_h,
    up_h,
    value_h,
    igrad_h,
    dgrad_h,
    ugrad_h,
    act,
    dy_raw,
    dy_blocks,
    weights,
    down,
    up,
    low,
    in_wide,
    back_wide,
    dpart,
    dsum,
    upart,
    usum,
    vpart,
    vsend,
    vrecv,
    vout,
    igacc,
    igout,
    local_sem,
    out_sem,
    own_send,
    z_send,
    z_recv,
    y_send,
    y_recv,
    ca_send,
    ca_recv,
    cb_send,
    cb_recv,
    x_send,
    x_recv,
    v_send,
    v_recv,
    r_send,
    r_recv,
):
    g = lax.axis_index("groups")
    f = lax.axis_index("fsdp")
    s = lax.axis_index("sub")
    r = lax.axis_index("rep")
    fsdp = 4
    slots = lengths.shape[0]
    rows, feats = act.shape
    tile = rows // slots
    block = w_h.shape[0]
    quarter = feats // 4
    width = quarter // CHUNKS
    to_y = {"groups": 1 - g}
    to_x = {"sub": 1 - s}
    to_r = {"rep": 1 - r}
    to_lo = {"fsdp": jnp.maximum(f - 1, 0)}
    to_hi = {"fsdp": jnp.minimum(f + 1, fsdp - 1)}

    barrier = pltpu.get_barrier_semaphore()
    for peer in (to_y, to_x, to_r):
        pl.semaphore_signal(barrier, inc=1, device_id=peer, device_id_type=pl.DeviceIdType.MESH)

    @pl.when(f > 0)
    def _():
        pl.semaphore_signal(barrier, inc=1, device_id=to_lo, device_id_type=pl.DeviceIdType.MESH)

    @pl.when(f < fsdp - 1)
    def _():
        pl.semaphore_signal(barrier, inc=1, device_id=to_hi, device_id_type=pl.DeviceIdType.MESH)

    local = [
        pltpu.make_async_copy(src, dst, local_sem.at[i])
        for i, (src, dst) in enumerate(
            (
                (act_h, act),
                (down_h, down),
                (w_h, weights.at[f]),
                (dy_h, dy_raw.at[s]),
                (up_h, up.at[s]),
            )
        )
    ]
    for copy in local:
        copy.start()
    ends = jnp.where(f == 0, 1, 0) + jnp.where(f == fsdp - 1, 1, 0)
    pl.semaphore_wait(barrier, 5 - ends)

    def remote(src, dst, send, recv, peer):
        return pltpu.make_async_remote_copy(
            src_ref=src,
            dst_ref=dst,
            send_sem=send,
            recv_sem=recv,
            device_id=peer,
            device_id_type=pl.DeviceIdType.MESH,
        )

    def columns(gg, rr, c):
        return pl.ds(pl.multiple_of((gg * 2 + rr) * quarter + c * width, width), width)

    def own_copy(c, down_way):
        cols = columns(g, r, c)
        return remote(
            w_h.at[:, cols],
            weights.at[f, :, cols],
            own_send.at[0 if down_way else 1, c],
            z_recv.at[f, c],
            to_lo if down_way else to_hi,
        )

    for c in range(CHUNKS):

        @pl.when(f > 0)
        def _():
            own_copy(c, True).start()

        @pl.when(f < fsdp - 1)
        def _():
            own_copy(c, False).start()

    x_dy = remote(dy_h, dy_raw.at[s], x_send.at[0], x_recv.at[0], to_x)
    x_up = remote(up_h, up.at[s], x_send.at[1], x_recv.at[1], to_x)
    x_low = remote(low.at[s], low.at[s], x_send.at[2], x_recv.at[2], to_x)
    x_up.start()
    x_dy.start()

    order = ((1, 2, 3), (2, 0, 3), (1, 3, 0), (2, 1, 0))
    arrivals = []
    for t in range(fsdp - 1):
        j = jnp.int32(order[0][t])
        for p in range(1, fsdp):
            j = jnp.where(f == p, order[p][t], j)
        arrivals.append(j)

    def piece(j, gg, rr, c):
        return weights.at[j, :, columns(gg, rr, c)]

    def z_copy(j, c, peer):
        here = piece(j, g, r, c)
        return remote(here, here, z_send.at[j, c], z_recv.at[j, c], peer)

    def y_copy(j, c):
        here = piece(j, g, r, c)
        return remote(here, here, y_send.at[j, c], y_recv.at[j, c], to_y)

    def ca_copy(j, c):
        here = piece(j, g, r, c)
        return remote(here, here, ca_send.at[j, c], ca_recv.at[j, c], to_r)

    def cb_copy(j, c):
        here = piece(j, 1 - g, r, c)
        return remote(here, here, cb_send.at[j, c], cb_recv.at[j, c], to_r)

    def step(i):
        j, c = arrivals[i // CHUNKS], i % CHUNKS
        z_copy(j, c, to_y).wait_recv()

        @pl.when((j > f) & (f > 0))
        def _():
            z_copy(j, c, to_lo).start()

        @pl.when((j < f) & (f < fsdp - 1))
        def _():
            z_copy(j, c, to_hi).start()

        y_copy(j, c).start()
        ca_copy(j, c).start()

    def y_step(i):
        j, c = arrivals[i // CHUNKS], i % CHUNKS
        here = piece(j, 1 - g, r, c)
        remote(here, here, y_send.at[j, c], y_recv.at[j, c], to_y).wait_recv()
        cb_copy(j, c).start()

    def both(i):
        step(i)
        y_step(i - 1)

    def core_wait(t):
        j = arrivals[t]
        for c in range(CHUNKS):
            here = piece(j, g, 1 - r, c)
            remote(here, here, ca_send.at[j, c], ca_recv.at[j, c], to_r).wait_recv()
            here = piece(j, 1 - g, 1 - r, c)
            remote(here, here, cb_send.at[j, c], cb_recv.at[j, c], to_r).wait_recv()

    own_count = counts[f * 2 + r]

    def valid(i, lanes):
        used = jnp.where(i < own_count, lengths[i], 0)
        return lax.broadcasted_iota(jnp.int32, (tile, lanes), 0) < used

    def chosen(i):
        lanes = lax.broadcasted_iota(jnp.int32, (tile, down.shape[0]), 1)
        return lanes // (down.shape[0] // 2) == picks[i]

    def tiles(i):
        return slice(i * tile, (i + 1) * tile)

    def v_copy(q):
        return remote(vsend.at[q], vrecv.at[q], v_send.at[q], v_recv.at[q], to_x)

    def value_block(j):
        part = dot_nt(act[...], weights[j])
        vpart[j] = part

        @pl.when(j // 2 != s)
        def _():
            q = j % 2
            vsend[q] = part.astype(jnp.bfloat16)
            v_copy(q).start()

    step_cols = 512

    def grad_block(j):
        @pl.loop(0, feats // step_cols)
        def _(k):
            cols = pl.ds(pl.multiple_of(k * step_cols, step_cols), step_cols)
            igacc[:, cols] += dot_nn(dy_blocks[j], weights[j, :, cols])

    local[0].wait()
    local[1].wait()
    wide = dot_nt(act[...], down[...])
    for i in range(slots):
        low[s, tiles(i), :] = jnp.where(chosen(i), wide[tiles(i), :], 0.0)
    x_low.start()
    local[2].wait()
    value_block(f)
    step(0)
    both(1)
    local[3].wait()
    local[4].wait()
    x_dy_in = remote(dy_raw.at[1 - s], dy_raw.at[1 - s], x_send.at[0], x_recv.at[0], to_x)
    x_up_in = remote(up.at[1 - s], up.at[1 - s], x_send.at[1], x_recv.at[1], to_x)
    x_low_in = remote(low.at[1 - s], low.at[1 - s], x_send.at[2], x_recv.at[2], to_x)
    x_dy_in.wait_recv()
    x_up_in.wait_recv()
    for h in range(2):
        for q in range(2):
            for i in range(slots):
                raw = dy_raw[h, tiles(i), q * block : (q + 1) * block].astype(jnp.float32)
                dy_blocks[2 * h + q, tiles(i), :] = jnp.where(valid(i, block), raw, 0.0).astype(
                    jnp.bfloat16
                )
    both(2)
    back = dot_nt(dy_blocks[0], up[0, :, 0:block])
    for b in range(1, 4):
        q = b % 2
        back += dot_nt(dy_blocks[b], up[b // 2, :, q * block : (q + 1) * block])
    back = jnp.concatenate(
        [jnp.where(chosen(i), back[tiles(i), :], 0.0) for i in range(slots)], axis=0
    )
    back_wide[...] = back.astype(jnp.bfloat16)
    back_turned = back.T.astype(jnp.bfloat16)

    @pl.loop(0, feats // step_cols)
    def _(k):
        cols = pl.ds(pl.multiple_of(k * step_cols, step_cols), step_cols)
        dpart[r, :, cols] = adapter_scale * dot_nn(back_turned, act[:, cols])

    r_down = remote(dpart.at[r], dpart.at[r], r_send.at[0], r_recv.at[0], to_r)
    r_up = remote(upart.at[r], upart.at[r], r_send.at[1], r_recv.at[1], to_r)
    r_down.start()
    both(3)

    @pl.loop(0, feats // step_cols)
    def _(k):
        cols = pl.ds(pl.multiple_of(k * step_cols, step_cols), step_cols)
        igacc[:, cols] = dot_nn(dy_blocks[f], weights[f, :, cols]) + adapter_scale * dot_nn(
            back_wide[...], down[:, cols]
        )

    both(4)
    x_low_in.wait_recv()
    total = low[0] + low[1]
    in_wide[...] = total.astype(jnp.bfloat16)
    turned = total.T.astype(jnp.bfloat16)
    for q in range(2):
        upart[r, :, q * block : (q + 1) * block] = adapter_scale * dot_nn(
            turned, dy_blocks[2 * s + q]
        )
    r_up.start()
    core_wait(0)
    value_block(arrivals[0])
    both(5)
    grad_block(arrivals[0])
    both(6)
    remote(dpart.at[1 - r], dpart.at[1 - r], r_send.at[0], r_recv.at[0], to_r).wait_recv()
    dsum[...] = (dpart[0] + dpart[1]).astype(jnp.bfloat16)
    out_down = pltpu.make_async_copy(dsum, dgrad_h, out_sem.at[0])
    out_down.start()
    both(7)
    remote(upart.at[1 - r], upart.at[1 - r], r_send.at[1], r_recv.at[1], to_r).wait_recv()
    usum[...] = (upart[0] + upart[1]).astype(jnp.bfloat16)
    out_up = pltpu.make_async_copy(usum, ugrad_h, out_sem.at[1])
    out_up.start()
    both(8)
    core_wait(1)
    value_block(arrivals[1])
    both(9)
    grad_block(arrivals[1])
    both(10)
    both(11)
    y_step(11)
    core_wait(2)
    last = arrivals[2]
    value_block(last)

    def out_grad(k):
        cols = pl.ds(pl.multiple_of(k * step_cols, step_cols), step_cols)
        return pltpu.make_async_copy(igout.at[:, cols], igrad_h.at[:, cols], out_sem.at[3 + k])

    @pl.loop(0, feats // step_cols)
    def _(k):
        cols = pl.ds(pl.multiple_of(k * step_cols, step_cols), step_cols)
        igout[:, cols] = (igacc[:, cols] + dot_nn(dy_blocks[last], weights[last, :, cols])).astype(
            jnp.bfloat16
        )
        out_grad(k).start()

    for q in range(2):
        v_copy(q).wait_recv()
        extra = dot_nn(in_wide[...], up[s, :, q * block : (q + 1) * block])
        for i in range(slots):
            v = (
                vpart[2 * s + q, tiles(i), :]
                + vrecv[q, tiles(i), :].astype(jnp.float32)
                + adapter_scale * extra[tiles(i), :]
            )
            vout[tiles(i), q * block : (q + 1) * block] = jnp.where(valid(i, block), v, 0.0).astype(
                jnp.bfloat16
            )
    out_value = pltpu.make_async_copy(vout, value_h, out_sem.at[2])
    out_value.start()

    for c in range(CHUNKS):

        @pl.when(f > 0)
        def _():
            own_copy(c, True).wait_send()

        @pl.when(f < fsdp - 1)
        def _():
            own_copy(c, False).wait_send()

        for j in arrivals:

            @pl.when((j > f) & (f > 0))
            def _():
                z_copy(j, c, to_lo).wait_send()

            @pl.when((j < f) & (f < fsdp - 1))
            def _():
                z_copy(j, c, to_hi).wait_send()

            y_copy(j, c).wait_send()
            ca_copy(j, c).wait_send()
            cb_copy(j, c).wait_send()
    x_dy.wait_send()
    x_up.wait_send()
    x_low.wait_send()
    r_down.wait_send()
    r_up.wait_send()
    for q in range(2):
        v_copy(q).wait_send()
    for k in range(feats // step_cols):
        out_grad(k).wait()
    out_down.wait()
    out_up.wait()
    out_value.wait()


def on_device(
    activations,
    cotangent,
    base_weight,
    adapter_down,
    adapter_up,
    tile_counts,
    tile_length,
    tile_adapter,
):
    rows, feats = activations.shape
    heads = cotangent.shape[1]
    sets, low_rank = adapter_up.shape[:2]
    ranks = sets * low_rank
    block = base_weight.shape[0]
    down = adapter_down.transpose(0, 2, 1).reshape(ranks, feats)
    up = adapter_up.reshape(ranks, heads)
    bf16, f32 = jnp.bfloat16, jnp.float32
    dma = pltpu.SemaphoreType.DMA
    whole = pl.BlockSpec(memory_space=pl.ANY)
    scalars = pl.BlockSpec(memory_space=pltpu.SMEM)
    value, igrad, dgrad, ugrad = pl.pallas_call(
        fused_kernel,
        out_shape=(
            jax.ShapeDtypeStruct((rows, heads), bf16),
            jax.ShapeDtypeStruct((rows, feats), bf16),
            jax.ShapeDtypeStruct((ranks, feats), bf16),
            jax.ShapeDtypeStruct((ranks, heads), bf16),
        ),
        in_specs=[scalars] * 3 + [whole] * 5,
        out_specs=(whole,) * 4,
        scratch_shapes=[
            pltpu.VMEM((rows, feats), bf16),
            pltpu.VMEM((2, rows, heads), bf16),
            pltpu.VMEM((4, rows, block), bf16),
            pltpu.VMEM((4, block, feats), bf16),
            pltpu.VMEM((ranks, feats), bf16),
            pltpu.VMEM((2, ranks, heads), bf16),
            pltpu.VMEM((2, rows, ranks), f32),
            pltpu.VMEM((rows, ranks), bf16),
            pltpu.VMEM((rows, ranks), bf16),
            pltpu.VMEM((2, ranks, feats), f32),
            pltpu.VMEM((ranks, feats), bf16),
            pltpu.VMEM((2, ranks, heads), f32),
            pltpu.VMEM((ranks, heads), bf16),
            pltpu.VMEM((4, rows, block), f32),
            pltpu.VMEM((2, rows, block), bf16),
            pltpu.VMEM((2, rows, block), bf16),
            pltpu.VMEM((rows, heads), bf16),
            pltpu.VMEM((rows, feats), f32),
            pltpu.VMEM((rows, feats), bf16),
            dma((5,)),
            dma((3 + feats // 512,)),
            dma((2, CHUNKS)),
        ]
        + [dma((4, CHUNKS))] * 8
        + [dma((3,)), dma((3,)), dma((2,)), dma((2,)), dma((2,)), dma((2,))],
        compiler_params=pltpu.CompilerParams(
            collective_id=0, has_side_effects=True, vmem_limit_bytes=60 * 1024 * 1024
        ),
    )(tile_counts, tile_length, tile_adapter, activations, cotangent, base_weight, down, up)
    return (
        value,
        igrad,
        dgrad.reshape(sets, low_rank, feats).transpose(0, 2, 1),
        ugrad.reshape(sets, low_rank, heads),
    )


def solution(mesh):
    sizes = (mesh.shape["groups"], mesh.shape["fsdp"], mesh.shape["sub"], mesh.shape["rep"])
    return jax.shard_map(
        on_device if sizes == (2, 4, 2, 2) else on_device_general,
        mesh=mesh,
        in_specs=(
            P(("groups", "fsdp", "rep"), "sub"),
            P(("groups", "fsdp", "rep"), "sub"),
            P("fsdp", "sub"),
            P(("groups", "fsdp"), "sub", None),
            P(("groups", "fsdp"), None, "sub"),
            P("groups"),
            P(("groups", "fsdp", "rep")),
            P(("groups", "fsdp", "rep")),
        ),
        out_specs=(
            P(("groups", "fsdp", "rep"), "sub"),
            P(("groups", "fsdp", "rep"), "sub"),
            P(("groups", "fsdp"), "sub", None),
            P(("groups", "fsdp"), None, "sub"),
        ),
        check_vma=False,
    )
```

```python
import functools

import jax
import jax.numpy as jnp
from jax import lax
from jax.experimental import pallas as pl
from jax.experimental.pallas import tpu as pltpu
from jax.sharding import PartitionSpec as P

adapter_scale = 2.0


def on_device_general(
    activations,
    cotangent,
    base_weight,
    adapter_down,
    adapter_up,
    tile_counts,
    tile_length,
    tile_adapter,
):
    slot_count = tile_length.shape[0]
    tile_rows = activations.shape[0] // slot_count
    feat_width = activations.shape[1]
    head_width = cotangent.shape[1]
    own_sets = adapter_down.shape[0]
    low_rank = adapter_down.shape[2]
    rep_count = lax.axis_size("rep")
    fsdp_pos = lax.axis_index("fsdp")
    rep_pos = lax.axis_index("rep")
    own_count = tile_counts[fsdp_pos * rep_count + rep_pos]
    slot_ids = jnp.arange(slot_count, dtype=jnp.int32)
    positions = jnp.arange(tile_rows, dtype=jnp.int32)
    row_valid = (
        (slot_ids < own_count)[:, None] & (positions[None, :] < tile_length[:, None])
    ).astype(jnp.bfloat16)
    masked_dy = cotangent.reshape(slot_count, tile_rows, head_width) * row_valid[:, :, None]
    adapter_pick = (tile_adapter[:, None] == jnp.arange(own_sets, dtype=jnp.int32)[None, :]).astype(
        jnp.bfloat16
    )
    contract_last = (((1,), (1,)), ((), ()))
    contract_first = (((0,), (0,)), ((), ()))
    valid_rows = row_valid.reshape(-1)[:, None].astype(jnp.float32)
    work_dy = masked_dy.reshape(-1, head_width)
    row_count = activations.shape[0]
    set_count = adapter_down.shape[0]
    chosen_rows = jnp.broadcast_to(
        adapter_pick[:, None, :], (adapter_pick.shape[0], tile_rows, set_count)
    ).reshape(row_count, set_count)
    flattened_down = adapter_down.transpose(1, 0, 2).reshape(feat_width, set_count * low_rank)
    flat_up = adapter_up.reshape(set_count * low_rank, head_width)
    pick_adapter_rows = chosen_rows.astype(jnp.float32)[:, :, None]
    adapter_input_grad = jnp.dot(
        activations, flattened_down, preferred_element_type=jnp.float32
    ).reshape(row_count, set_count, low_rank)
    adapter_backward = lax.dot_general(
        work_dy, flat_up, contract_last, preferred_element_type=jnp.float32
    ).reshape(row_count, set_count, low_rank)
    input_piece = jnp.sum(adapter_input_grad * pick_adapter_rows, axis=1)
    backward_piece = jnp.sum(adapter_backward * pick_adapter_rows, axis=1)
    in_sum, back_sum = lax.psum((input_piece, backward_piece), "sub")
    in_low = in_sum.astype(jnp.bfloat16)
    back_low = back_sum.astype(jnp.bfloat16)
    in_wide = (chosen_rows[:, :, None] * in_low[:, None, :]).reshape(
        row_count, set_count * low_rank
    )
    back_wide = (chosen_rows[:, :, None] * back_low[:, None, :]).reshape(
        row_count, set_count * low_rank
    )
    full_dy = lax.all_gather(work_dy, "sub", axis=1, tiled=True)
    whole_weight = lax.all_gather(base_weight, "fsdp", axis=0, tiled=True)
    value_part = lax.dot_general(
        activations, whole_weight, contract_last, preferred_element_type=jnp.float32
    )
    input_frozen_grad = jnp.dot(full_dy, whole_weight, preferred_element_type=jnp.float32)
    value_frozen_out = lax.psum_scatter(value_part, "sub", scatter_dimension=1, tiled=True)
    value_total_out = value_frozen_out + adapter_scale * jnp.dot(
        in_wide, flat_up, preferred_element_type=jnp.float32
    )
    input_total_grad = input_frozen_grad + adapter_scale * lax.dot_general(
        back_wide, flattened_down, contract_last, preferred_element_type=jnp.float32
    )
    down_product = adapter_scale * lax.dot_general(
        activations, back_wide, contract_first, preferred_element_type=jnp.float32
    )
    up_product = adapter_scale * lax.dot_general(
        in_wide, work_dy, contract_first, preferred_element_type=jnp.float32
    )
    down_product = down_product.reshape(feat_width, set_count, low_rank).transpose(1, 0, 2)
    up_product = up_product.reshape(set_count, low_rank, head_width)
    value_total_out, input_total_grad, down_grad, up_grad = (
        value_total_out,
        input_total_grad,
        down_product,
        up_product,
    )
    down_total, up_total = lax.psum((down_grad, up_grad), "rep")
    value_proj = (value_total_out * valid_rows).astype(jnp.bfloat16)
    return (
        value_proj,
        input_total_grad.astype(jnp.bfloat16),
        down_total.astype(jnp.bfloat16),
        up_total.astype(jnp.bfloat16),
    )


CHUNKS = 4
NT = (((1,), (1,)), ((), ()))


def dot_nt(a, b):
    return lax.dot_general(a, b, NT, preferred_element_type=jnp.float32)


def dot_nn(a, b):
    return jnp.dot(a, b, preferred_element_type=jnp.float32)


def fused_kernel(
    counts,
    lengths,
    picks,
    act_h,
    dy_h,
    w_h,
    down_h,
    up_h,
    value_h,
    igrad_h,
    dgrad_h,
    ugrad_h,
    act,
    dy_raw,
    dy_blocks,
    weights,
    down,
    up,
    low,
    in_wide,
    back_wide,
    dpart,
    dsum,
    upart,
    usum,
    vpart,
    vsend,
    vrecv,
    vout,
    igacc,
    igout,
    local_sem,
    out_sem,
    own_send,
    z_send,
    z_recv,
    y_send,
    y_recv,
    ca_send,
    ca_recv,
    cb_send,
    cb_recv,
    x_send,
    x_recv,
    v_send,
    v_recv,
    r_send,
    r_recv,
):
    g = lax.axis_index("groups")
    f = lax.axis_index("fsdp")
    s = lax.axis_index("sub")
    r = lax.axis_index("rep")
    fsdp = 4
    slots = lengths.shape[0]
    rows, feats = act.shape
    tile = rows // slots
    block = w_h.shape[0]
    quarter = feats // 4
    width = quarter // CHUNKS
    to_y = {"groups": 1 - g}
    to_x = {"sub": 1 - s}
    to_r = {"rep": 1 - r}
    to_lo = {"fsdp": jnp.maximum(f - 1, 0)}
    to_hi = {"fsdp": jnp.minimum(f + 1, fsdp - 1)}

    barrier = pltpu.get_barrier_semaphore()
    for peer in (to_y, to_x, to_r):
        pl.semaphore_signal(barrier, inc=1, device_id=peer, device_id_type=pl.DeviceIdType.MESH)

    @pl.when(f > 0)
    def _():
        pl.semaphore_signal(barrier, inc=1, device_id=to_lo, device_id_type=pl.DeviceIdType.MESH)

    @pl.when(f < fsdp - 1)
    def _():
        pl.semaphore_signal(barrier, inc=1, device_id=to_hi, device_id_type=pl.DeviceIdType.MESH)

    local = [
        pltpu.make_async_copy(src, dst, local_sem.at[i])
        for i, (src, dst) in enumerate(
            (
                (act_h, act),
                (down_h, down),
                (w_h, weights.at[f]),
                (dy_h, dy_raw.at[s]),
                (up_h, up.at[s]),
            )
        )
    ]
    for copy in local:
        copy.start()
    ends = jnp.where(f == 0, 1, 0) + jnp.where(f == fsdp - 1, 1, 0)
    pl.semaphore_wait(barrier, 5 - ends)

    def remote(src, dst, send, recv, peer):
        return pltpu.make_async_remote_copy(
            src_ref=src,
            dst_ref=dst,
            send_sem=send,
            recv_sem=recv,
            device_id=peer,
            device_id_type=pl.DeviceIdType.MESH,
        )

    def columns(gg, rr, c):
        return pl.ds(pl.multiple_of((gg * 2 + rr) * quarter + c * width, width), width)

    def own_copy(c, down_way):
        cols = columns(g, r, c)
        return remote(
            w_h.at[:, cols],
            weights.at[f, :, cols],
            own_send.at[0 if down_way else 1, c],
            z_recv.at[f, c],
            to_lo if down_way else to_hi,
        )

    for c in range(CHUNKS):

        @pl.when(f > 0)
        def _():
            own_copy(c, True).start()

        @pl.when(f < fsdp - 1)
        def _():
            own_copy(c, False).start()

    x_dy = remote(dy_h, dy_raw.at[s], x_send.at[0], x_recv.at[0], to_x)
    x_up = remote(up_h, up.at[s], x_send.at[1], x_recv.at[1], to_x)
    x_low = remote(low.at[s], low.at[s], x_send.at[2], x_recv.at[2], to_x)
    x_up.start()
    x_dy.start()

    order = ((1, 2, 3), (2, 0, 3), (1, 3, 0), (2, 1, 0))
    arrivals = []
    for t in range(fsdp - 1):
        j = jnp.int32(order[0][t])
        for p in range(1, fsdp):
            j = jnp.where(f == p, order[p][t], j)
        arrivals.append(j)

    def piece(j, gg, rr, c):
        return weights.at[j, :, columns(gg, rr, c)]

    def z_copy(j, c, peer):
        here = piece(j, g, r, c)
        return remote(here, here, z_send.at[j, c], z_recv.at[j, c], peer)

    def y_copy(j, c):
        here = piece(j, g, r, c)
        return remote(here, here, y_send.at[j, c], y_recv.at[j, c], to_y)

    def ca_copy(j, c):
        here = piece(j, g, r, c)
        return remote(here, here, ca_send.at[j, c], ca_recv.at[j, c], to_r)

    def cb_copy(j, c):
        here = piece(j, 1 - g, r, c)
        return remote(here, here, cb_send.at[j, c], cb_recv.at[j, c], to_r)

    def step(i):
        j, c = arrivals[i // CHUNKS], i % CHUNKS
        z_copy(j, c, to_y).wait_recv()

        @pl.when((j > f) & (f > 0))
        def _():
            z_copy(j, c, to_lo).start()

        @pl.when((j < f) & (f < fsdp - 1))
        def _():
            z_copy(j, c, to_hi).start()

        y_copy(j, c).start()
        ca_copy(j, c).start()

    def y_step(i):
        j, c = arrivals[i // CHUNKS], i % CHUNKS
        here = piece(j, 1 - g, r, c)
        remote(here, here, y_send.at[j, c], y_recv.at[j, c], to_y).wait_recv()
        cb_copy(j, c).start()

    def both(i):
        step(i)
        y_step(i - 1)

    def core_wait(t):
        j = arrivals[t]
        for c in range(CHUNKS):
            here = piece(j, g, 1 - r, c)
            remote(here, here, ca_send.at[j, c], ca_recv.at[j, c], to_r).wait_recv()
            here = piece(j, 1 - g, 1 - r, c)
            remote(here, here, cb_send.at[j, c], cb_recv.at[j, c], to_r).wait_recv()

    own_count = counts[f * 2 + r]

    def valid(i, lanes):
        used = jnp.where(i < own_count, lengths[i], 0)
        return lax.broadcasted_iota(jnp.int32, (tile, lanes), 0) < used

    def chosen(i):
        lanes = lax.broadcasted_iota(jnp.int32, (tile, down.shape[0]), 1)
        return lanes // (down.shape[0] // 2) == picks[i]

    def tiles(i):
        return slice(i * tile, (i + 1) * tile)

    def v_copy(q):
        return remote(vsend.at[q], vrecv.at[q], v_send.at[q], v_recv.at[q], to_x)

    def value_block(j):
        part = dot_nt(act[...], weights[j])
        vpart[j] = part

        @pl.when(j // 2 != s)
        def _():
            q = j % 2
            vsend[q] = part.astype(jnp.bfloat16)
            v_copy(q).start()

    step_cols = 512

    half = feats // step_cols // 2

    def grad_block(j, part):
        @pl.loop(part * half, (part + 1) * half)
        def _(k):
            cols = pl.ds(pl.multiple_of(k * step_cols, step_cols), step_cols)
            igacc[:, cols] += dot_nn(dy_blocks[j], weights[j, :, cols])

    local[0].wait()
    local[1].wait()
    wide = dot_nt(act[...], down[...])
    for i in range(slots):
        low[s, tiles(i), :] = jnp.where(chosen(i), wide[tiles(i), :], 0.0)
    x_low.start()
    local[2].wait()
    value_block(f)
    step(0)
    both(1)
    local[3].wait()
    local[4].wait()
    x_dy_in = remote(dy_raw.at[1 - s], dy_raw.at[1 - s], x_send.at[0], x_recv.at[0], to_x)
    x_up_in = remote(up.at[1 - s], up.at[1 - s], x_send.at[1], x_recv.at[1], to_x)
    x_low_in = remote(low.at[1 - s], low.at[1 - s], x_send.at[2], x_recv.at[2], to_x)
    x_dy_in.wait_recv()
    x_up_in.wait_recv()
    for h in range(2):
        for q in range(2):
            for i in range(slots):
                raw = dy_raw[h, tiles(i), q * block : (q + 1) * block].astype(jnp.float32)
                dy_blocks[2 * h + q, tiles(i), :] = jnp.where(valid(i, block), raw, 0.0).astype(
                    jnp.bfloat16
                )
    both(2)
    back = dot_nt(dy_blocks[0], up[0, :, 0:block])
    for b in range(1, 4):
        q = b % 2
        back += dot_nt(dy_blocks[b], up[b // 2, :, q * block : (q + 1) * block])
    back = jnp.concatenate(
        [jnp.where(chosen(i), back[tiles(i), :], 0.0) for i in range(slots)], axis=0
    )
    back_wide[...] = back.astype(jnp.bfloat16)
    back_turned = back.T.astype(jnp.bfloat16)

    @pl.loop(0, feats // step_cols)
    def _(k):
        cols = pl.ds(pl.multiple_of(k * step_cols, step_cols), step_cols)
        dpart[r, :, cols] = adapter_scale * dot_nn(back_turned, act[:, cols])

    r_down = remote(dpart.at[r], dpart.at[r], r_send.at[0], r_recv.at[0], to_r)
    r_up = remote(upart.at[r], upart.at[r], r_send.at[1], r_recv.at[1], to_r)
    r_down.start()
    both(3)
    both(4)

    def first_grad(part):
        @pl.loop(part * half, (part + 1) * half)
        def _(k):
            cols = pl.ds(pl.multiple_of(k * step_cols, step_cols), step_cols)
            igacc[:, cols] = dot_nn(dy_blocks[f], weights[f, :, cols]) + adapter_scale * dot_nn(
                back_wide[...], down[:, cols]
            )

    first_grad(0)
    both(5)
    first_grad(1)
    both(6)
    x_low_in.wait_recv()
    total = low[0] + low[1]
    in_wide[...] = total.astype(jnp.bfloat16)
    turned = total.T.astype(jnp.bfloat16)
    for q in range(2):
        upart[r, :, q * block : (q + 1) * block] = adapter_scale * dot_nn(
            turned, dy_blocks[2 * s + q]
        )
    r_up.start()
    core_wait(0)
    value_block(arrivals[0])
    both(7)
    grad_block(arrivals[0], 0)
    both(8)
    grad_block(arrivals[0], 1)
    both(9)
    core_wait(1)
    value_block(arrivals[1])
    both(10)
    grad_block(arrivals[1], 0)
    both(11)
    grad_block(arrivals[1], 1)
    y_step(11)
    remote(dpart.at[1 - r], dpart.at[1 - r], r_send.at[0], r_recv.at[0], to_r).wait_recv()
    dsum[...] = (dpart[0] + dpart[1]).astype(jnp.bfloat16)
    out_down = pltpu.make_async_copy(dsum, dgrad_h, out_sem.at[0])
    out_down.start()
    remote(upart.at[1 - r], upart.at[1 - r], r_send.at[1], r_recv.at[1], to_r).wait_recv()
    usum[...] = (upart[0] + upart[1]).astype(jnp.bfloat16)
    out_up = pltpu.make_async_copy(usum, ugrad_h, out_sem.at[1])
    out_up.start()
    core_wait(2)
    last = arrivals[2]
    value_block(last)

    def out_grad(k):
        cols = pl.ds(pl.multiple_of(k * step_cols, step_cols), step_cols)
        return pltpu.make_async_copy(igout.at[:, cols], igrad_h.at[:, cols], out_sem.at[3 + k])

    @pl.loop(0, feats // step_cols)
    def _(k):
        cols = pl.ds(pl.multiple_of(k * step_cols, step_cols), step_cols)
        igout[:, cols] = (igacc[:, cols] + dot_nn(dy_blocks[last], weights[last, :, cols])).astype(
            jnp.bfloat16
        )
        out_grad(k).start()

    for q in range(2):
        v_copy(q).wait_recv()
        extra = dot_nn(in_wide[...], up[s, :, q * block : (q + 1) * block])
        for i in range(slots):
            v = (
                vpart[2 * s + q, tiles(i), :]
                + vrecv[q, tiles(i), :].astype(jnp.float32)
                + adapter_scale * extra[tiles(i), :]
            )
            vout[tiles(i), q * block : (q + 1) * block] = jnp.where(valid(i, block), v, 0.0).astype(
                jnp.bfloat16
            )
    out_value = pltpu.make_async_copy(vout, value_h, out_sem.at[2])
    out_value.start()

    for c in range(CHUNKS):

        @pl.when(f > 0)
        def _():
            own_copy(c, True).wait_send()

        @pl.when(f < fsdp - 1)
        def _():
            own_copy(c, False).wait_send()

        for j in arrivals:

            @pl.when((j > f) & (f > 0))
            def _():
                z_copy(j, c, to_lo).wait_send()

            @pl.when((j < f) & (f < fsdp - 1))
            def _():
                z_copy(j, c, to_hi).wait_send()

            y_copy(j, c).wait_send()
            ca_copy(j, c).wait_send()
            cb_copy(j, c).wait_send()
    x_dy.wait_send()
    x_up.wait_send()
    x_low.wait_send()
    r_down.wait_send()
    r_up.wait_send()
    for q in range(2):
        v_copy(q).wait_send()
    for k in range(feats // step_cols):
        out_grad(k).wait()
    out_down.wait()
    out_up.wait()
    out_value.wait()


def hand_on_kernel(*refs):
    parts, count = 8, 4
    sources, targets, held = refs[:count], refs[count : 2 * count], refs[2 * count : 3 * count]
    into, out = refs[3 * count :]

    def piece(i, k):
        size = sources[i].shape[0] // parts
        return pl.ds(k * size, size)

    def load(i, k):
        rows = piece(i, k)
        return pltpu.make_async_copy(sources[i].at[rows], held[i].at[rows], into.at[i, k])

    def store(i, k):
        rows = piece(i, k)
        return pltpu.make_async_copy(held[i].at[rows], targets[i].at[rows], out.at[i, k])

    every = [(i, k) for i in range(count) for k in range(parts)]
    for i, k in every:
        load(i, k).start()
    for i, k in every:
        load(i, k).wait()
        store(i, k).start()
    for i, k in every:
        store(i, k).wait()


def on_device(
    activations,
    cotangent,
    base_weight,
    adapter_down,
    adapter_up,
    tile_counts,
    tile_length,
    tile_adapter,
):
    rows, feats = activations.shape
    heads = cotangent.shape[1]
    sets, low_rank = adapter_up.shape[:2]
    ranks = sets * low_rank
    block = base_weight.shape[0]
    down = adapter_down.transpose(0, 2, 1).reshape(ranks, feats)
    up = adapter_up.reshape(ranks, heads)
    bf16, f32 = jnp.bfloat16, jnp.float32
    dma = pltpu.SemaphoreType.DMA
    whole = pl.BlockSpec(memory_space=pl.ANY)
    scalars = pl.BlockSpec(memory_space=pltpu.SMEM)
    value, igrad, dgrad, ugrad = pl.pallas_call(
        fused_kernel,
        out_shape=(
            jax.ShapeDtypeStruct((rows, heads), bf16),
            jax.ShapeDtypeStruct((rows, feats), bf16),
            jax.ShapeDtypeStruct((ranks, feats), bf16),
            jax.ShapeDtypeStruct((ranks, heads), bf16),
        ),
        in_specs=[scalars] * 3 + [whole] * 5,
        out_specs=(whole,) * 4,
        scratch_shapes=[
            pltpu.VMEM((rows, feats), bf16),
            pltpu.VMEM((2, rows, heads), bf16),
            pltpu.VMEM((4, rows, block), bf16),
            pltpu.VMEM((4, block, feats), bf16),
            pltpu.VMEM((ranks, feats), bf16),
            pltpu.VMEM((2, ranks, heads), bf16),
            pltpu.VMEM((2, rows, ranks), f32),
            pltpu.VMEM((rows, ranks), bf16),
            pltpu.VMEM((rows, ranks), bf16),
            pltpu.VMEM((2, ranks, feats), f32),
            pltpu.VMEM((ranks, feats), bf16),
            pltpu.VMEM((2, ranks, heads), f32),
            pltpu.VMEM((ranks, heads), bf16),
            pltpu.VMEM((4, rows, block), f32),
            pltpu.VMEM((2, rows, block), bf16),
            pltpu.VMEM((2, rows, block), bf16),
            pltpu.VMEM((rows, heads), bf16),
            pltpu.VMEM((rows, feats), f32),
            pltpu.VMEM((rows, feats), bf16),
            dma((5,)),
            dma((3 + feats // 512,)),
            dma((2, CHUNKS)),
        ]
        + [dma((4, CHUNKS))] * 8
        + [dma((3,)), dma((3,)), dma((2,)), dma((2,)), dma((2,)), dma((2,))],
        compiler_params=pltpu.CompilerParams(
            collective_id=0, has_side_effects=True, vmem_limit_bytes=60 * 1024 * 1024
        ),
    )(tile_counts, tile_length, tile_adapter, activations, cotangent, base_weight, down, up)
    results = (value, igrad, dgrad, ugrad)
    value, igrad, dgrad, ugrad = pl.pallas_call(
        hand_on_kernel,
        out_shape=tuple(jax.ShapeDtypeStruct(a.shape, a.dtype) for a in results),
        in_specs=[whole] * 4,
        out_specs=(whole,) * 4,
        scratch_shapes=[pltpu.VMEM(a.shape, a.dtype) for a in results] + [dma((4, 8)), dma((4, 8))],
        compiler_params=pltpu.CompilerParams(vmem_limit_bytes=60 * 1024 * 1024),
    )(*results)
    return (
        value,
        igrad,
        dgrad.reshape(sets, low_rank, feats).transpose(0, 2, 1),
        ugrad.reshape(sets, low_rank, heads),
    )


def solution(mesh):
    sizes = (mesh.shape["groups"], mesh.shape["fsdp"], mesh.shape["sub"], mesh.shape["rep"])
    return jax.shard_map(
        on_device if sizes == (2, 4, 2, 2) else on_device_general,
        mesh=mesh,
        in_specs=(
            P(("groups", "fsdp", "rep"), "sub"),
            P(("groups", "fsdp", "rep"), "sub"),
            P("fsdp", "sub"),
            P(("groups", "fsdp"), "sub", None),
            P(("groups", "fsdp"), None, "sub"),
            P("groups"),
            P(("groups", "fsdp", "rep")),
            P(("groups", "fsdp", "rep")),
        ),
        out_specs=(
            P(("groups", "fsdp", "rep"), "sub"),
            P(("groups", "fsdp", "rep"), "sub"),
            P(("groups", "fsdp"), "sub", None),
            P(("groups", "fsdp"), None, "sub"),
        ),
        check_vma=False,
    )
```

```python
import functools

import jax
import jax.numpy as jnp
from jax import lax
from jax.experimental import pallas as pl
from jax.experimental.pallas import tpu as pltpu
from jax.sharding import PartitionSpec as P

adapter_scale = 2.0


def on_device_general(
    activations,
    cotangent,
    base_weight,
    adapter_down,
    adapter_up,
    tile_counts,
    tile_length,
    tile_adapter,
):
    slot_count = tile_length.shape[0]
    tile_rows = activations.shape[0] // slot_count
    feat_width = activations.shape[1]
    head_width = cotangent.shape[1]
    own_sets = adapter_down.shape[0]
    low_rank = adapter_down.shape[2]
    rep_count = lax.axis_size("rep")
    fsdp_pos = lax.axis_index("fsdp")
    rep_pos = lax.axis_index("rep")
    own_count = tile_counts[fsdp_pos * rep_count + rep_pos]
    slot_ids = jnp.arange(slot_count, dtype=jnp.int32)
    positions = jnp.arange(tile_rows, dtype=jnp.int32)
    row_valid = (
        (slot_ids < own_count)[:, None] & (positions[None, :] < tile_length[:, None])
    ).astype(jnp.bfloat16)
    masked_dy = cotangent.reshape(slot_count, tile_rows, head_width) * row_valid[:, :, None]
    adapter_pick = (tile_adapter[:, None] == jnp.arange(own_sets, dtype=jnp.int32)[None, :]).astype(
        jnp.bfloat16
    )
    contract_last = (((1,), (1,)), ((), ()))
    contract_first = (((0,), (0,)), ((), ()))
    valid_rows = row_valid.reshape(-1)[:, None].astype(jnp.float32)
    work_dy = masked_dy.reshape(-1, head_width)
    row_count = activations.shape[0]
    set_count = adapter_down.shape[0]
    chosen_rows = jnp.broadcast_to(
        adapter_pick[:, None, :], (adapter_pick.shape[0], tile_rows, set_count)
    ).reshape(row_count, set_count)
    flattened_down = adapter_down.transpose(1, 0, 2).reshape(feat_width, set_count * low_rank)
    flat_up = adapter_up.reshape(set_count * low_rank, head_width)
    pick_adapter_rows = chosen_rows.astype(jnp.float32)[:, :, None]
    adapter_input_grad = jnp.dot(
        activations, flattened_down, preferred_element_type=jnp.float32
    ).reshape(row_count, set_count, low_rank)
    adapter_backward = lax.dot_general(
        work_dy, flat_up, contract_last, preferred_element_type=jnp.float32
    ).reshape(row_count, set_count, low_rank)
    input_piece = jnp.sum(adapter_input_grad * pick_adapter_rows, axis=1)
    backward_piece = jnp.sum(adapter_backward * pick_adapter_rows, axis=1)
    in_sum, back_sum = lax.psum((input_piece, backward_piece), "sub")
    in_low = in_sum.astype(jnp.bfloat16)
    back_low = back_sum.astype(jnp.bfloat16)
    in_wide = (chosen_rows[:, :, None] * in_low[:, None, :]).reshape(
        row_count, set_count * low_rank
    )
    back_wide = (chosen_rows[:, :, None] * back_low[:, None, :]).reshape(
        row_count, set_count * low_rank
    )
    full_dy = lax.all_gather(work_dy, "sub", axis=1, tiled=True)
    whole_weight = lax.all_gather(base_weight, "fsdp", axis=0, tiled=True)
    value_part = lax.dot_general(
        activations, whole_weight, contract_last, preferred_element_type=jnp.float32
    )
    input_frozen_grad = jnp.dot(full_dy, whole_weight, preferred_element_type=jnp.float32)
    value_frozen_out = lax.psum_scatter(value_part, "sub", scatter_dimension=1, tiled=True)
    value_total_out = value_frozen_out + adapter_scale * jnp.dot(
        in_wide, flat_up, preferred_element_type=jnp.float32
    )
    input_total_grad = input_frozen_grad + adapter_scale * lax.dot_general(
        back_wide, flattened_down, contract_last, preferred_element_type=jnp.float32
    )
    down_product = adapter_scale * lax.dot_general(
        activations, back_wide, contract_first, preferred_element_type=jnp.float32
    )
    up_product = adapter_scale * lax.dot_general(
        in_wide, work_dy, contract_first, preferred_element_type=jnp.float32
    )
    down_product = down_product.reshape(feat_width, set_count, low_rank).transpose(1, 0, 2)
    up_product = up_product.reshape(set_count, low_rank, head_width)
    value_total_out, input_total_grad, down_grad, up_grad = (
        value_total_out,
        input_total_grad,
        down_product,
        up_product,
    )
    down_total, up_total = lax.psum((down_grad, up_grad), "rep")
    value_proj = (value_total_out * valid_rows).astype(jnp.bfloat16)
    return (
        value_proj,
        input_total_grad.astype(jnp.bfloat16),
        down_total.astype(jnp.bfloat16),
        up_total.astype(jnp.bfloat16),
    )


CHUNKS = 4
NT = (((1,), (1,)), ((), ()))


def dot_nt(a, b):
    return lax.dot_general(a, b, NT, preferred_element_type=jnp.float32)


def dot_nn(a, b):
    return jnp.dot(a, b, preferred_element_type=jnp.float32)


def fused_kernel(
    counts,
    lengths,
    picks,
    act_h,
    dy_h,
    w_h,
    down_h,
    up_h,
    value_h,
    igrad_h,
    dgrad_h,
    ugrad_h,
    act,
    dy_raw,
    dy_blocks,
    weights,
    down,
    up,
    low,
    in_wide,
    back_wide,
    dpart,
    dsum,
    upart,
    usum,
    vpart,
    vsend,
    vrecv,
    vout,
    igacc,
    igout,
    local_sem,
    out_sem,
    own_send,
    z_send,
    z_recv,
    y_send,
    y_recv,
    ca_send,
    ca_recv,
    cb_send,
    cb_recv,
    x_send,
    x_recv,
    v_send,
    v_recv,
    r_send,
    r_recv,
):
    g = lax.axis_index("groups")
    f = lax.axis_index("fsdp")
    s = lax.axis_index("sub")
    r = lax.axis_index("rep")
    fsdp = 4
    slots = lengths.shape[0]
    rows, feats = act.shape
    tile = rows // slots
    block = w_h.shape[0]
    quarter = feats // 4
    width = quarter // CHUNKS
    to_y = {"groups": 1 - g}
    to_x = {"sub": 1 - s}
    to_r = {"rep": 1 - r}
    to_lo = {"fsdp": jnp.maximum(f - 1, 0)}
    to_hi = {"fsdp": jnp.minimum(f + 1, fsdp - 1)}

    barrier = pltpu.get_barrier_semaphore()
    for peer in (to_y, to_x, to_r):
        pl.semaphore_signal(barrier, inc=1, device_id=peer, device_id_type=pl.DeviceIdType.MESH)

    @pl.when(f > 0)
    def _():
        pl.semaphore_signal(barrier, inc=1, device_id=to_lo, device_id_type=pl.DeviceIdType.MESH)

    @pl.when(f < fsdp - 1)
    def _():
        pl.semaphore_signal(barrier, inc=1, device_id=to_hi, device_id_type=pl.DeviceIdType.MESH)

    local = [
        pltpu.make_async_copy(src, dst, local_sem.at[i])
        for i, (src, dst) in enumerate(
            (
                (act_h, act),
                (down_h, down),
                (w_h, weights.at[f]),
                (dy_h, dy_raw.at[s]),
                (up_h, up.at[s]),
            )
        )
    ]
    for copy in local:
        copy.start()
    ends = jnp.where(f == 0, 1, 0) + jnp.where(f == fsdp - 1, 1, 0)
    pl.semaphore_wait(barrier, 5 - ends)

    def remote(src, dst, send, recv, peer):
        return pltpu.make_async_remote_copy(
            src_ref=src,
            dst_ref=dst,
            send_sem=send,
            recv_sem=recv,
            device_id=peer,
            device_id_type=pl.DeviceIdType.MESH,
        )

    def columns(gg, rr, c):
        return pl.ds(pl.multiple_of((gg * 2 + rr) * quarter + c * width, width), width)

    def own_copy(c, down_way):
        cols = columns(g, r, c)
        return remote(
            w_h.at[:, cols],
            weights.at[f, :, cols],
            own_send.at[0 if down_way else 1, c],
            z_recv.at[f, c],
            to_lo if down_way else to_hi,
        )

    for c in range(CHUNKS):

        @pl.when(f > 0)
        def _():
            own_copy(c, True).start()

        @pl.when(f < fsdp - 1)
        def _():
            own_copy(c, False).start()

    x_dy = remote(dy_h, dy_raw.at[s], x_send.at[0], x_recv.at[0], to_x)
    x_up = remote(up_h, up.at[s], x_send.at[1], x_recv.at[1], to_x)
    x_low = remote(low.at[s], low.at[s], x_send.at[2], x_recv.at[2], to_x)
    x_up.start()
    x_dy.start()

    order = ((1, 2, 3), (2, 0, 3), (1, 3, 0), (2, 1, 0))
    arrivals = []
    for t in range(fsdp - 1):
        j = jnp.int32(order[0][t])
        for p in range(1, fsdp):
            j = jnp.where(f == p, order[p][t], j)
        arrivals.append(j)

    def piece(j, gg, rr, c):
        return weights.at[j, :, columns(gg, rr, c)]

    def z_copy(j, c, peer):
        here = piece(j, g, r, c)
        return remote(here, here, z_send.at[j, c], z_recv.at[j, c], peer)

    def y_copy(j, c):
        here = piece(j, g, r, c)
        return remote(here, here, y_send.at[j, c], y_recv.at[j, c], to_y)

    def ca_copy(j, c):
        here = piece(j, g, r, c)
        return remote(here, here, ca_send.at[j, c], ca_recv.at[j, c], to_r)

    def cb_copy(j, c):
        here = piece(j, 1 - g, r, c)
        return remote(here, here, cb_send.at[j, c], cb_recv.at[j, c], to_r)

    def step(i):
        j, c = arrivals[i // CHUNKS], i % CHUNKS
        z_copy(j, c, to_y).wait_recv()

        @pl.when((j > f) & (f > 0))
        def _():
            z_copy(j, c, to_lo).start()

        @pl.when((j < f) & (f < fsdp - 1))
        def _():
            z_copy(j, c, to_hi).start()

        y_copy(j, c).start()
        ca_copy(j, c).start()

    def y_step(i):
        j, c = arrivals[i // CHUNKS], i % CHUNKS
        here = piece(j, 1 - g, r, c)
        remote(here, here, y_send.at[j, c], y_recv.at[j, c], to_y).wait_recv()
        cb_copy(j, c).start()

    def both(i):
        step(i)
        y_step(i - 1)

    def core_wait_chunk(t, c):
        j = arrivals[t]
        here = piece(j, g, 1 - r, c)
        remote(here, here, ca_send.at[j, c], ca_recv.at[j, c], to_r).wait_recv()
        here = piece(j, 1 - g, 1 - r, c)
        remote(here, here, cb_send.at[j, c], cb_recv.at[j, c], to_r).wait_recv()

    def core_wait(t):
        for c in range(CHUNKS):
            core_wait_chunk(t, c)

    own_count = counts[f * 2 + r]

    def valid(i, lanes):
        used = jnp.where(i < own_count, lengths[i], 0)
        return lax.broadcasted_iota(jnp.int32, (tile, lanes), 0) < used

    def chosen(i):
        lanes = lax.broadcasted_iota(jnp.int32, (tile, down.shape[0]), 1)
        return lanes // (down.shape[0] // 2) == picks[i]

    def tiles(i):
        return slice(i * tile, (i + 1) * tile)

    def v_copy(q):
        return remote(vsend.at[q], vrecv.at[q], v_send.at[q], v_recv.at[q], to_x)

    def value_block(j):
        part = dot_nt(act[...], weights[j])
        vpart[j] = part
        send_value(j, part)

    def send_value(j, part):
        @pl.when(j // 2 != s)
        def _():
            q = j % 2
            vsend[q] = part.astype(jnp.bfloat16)
            v_copy(q).start()

    step_cols = 512

    half = feats // step_cols // 2

    def grad_block(j, part):
        @pl.loop(part * half, (part + 1) * half)
        def _(k):
            cols = pl.ds(pl.multiple_of(k * step_cols, step_cols), step_cols)
            igacc[:, cols] += dot_nn(dy_blocks[j], weights[j, :, cols])

    last = arrivals[fsdp - 2]

    def out_grad(p, c):
        cols = pl.ds(p * quarter + c * width, width)
        return pltpu.make_async_copy(
            igout.at[:, cols], igrad_h.at[:, cols], out_sem.at[3 + p * CHUNKS + c]
        )

    def last_chunk(c):
        core_wait_chunk(fsdp - 2, c)
        part = vpart[last] if c > 0 else None
        for p in range(4):
            cols = slice(p * quarter + c * width, p * quarter + (c + 1) * width)
            term = dot_nt(act[:, cols], weights[last, :, cols])
            part = term if part is None else part + term
        vpart[last] = part
        if c == CHUNKS - 1:
            send_value(last, part)
        for p in range(4):
            cols = slice(p * quarter + c * width, p * quarter + (c + 1) * width)
            igout[:, cols] = (
                igacc[:, cols] + dot_nn(dy_blocks[last], weights[last, :, cols])
            ).astype(jnp.bfloat16)
            out_grad(p, c).start()

    local[0].wait()
    local[1].wait()
    wide = dot_nt(act[...], down[...])
    for i in range(slots):
        low[s, tiles(i), :] = jnp.where(chosen(i), wide[tiles(i), :], 0.0)
    x_low.start()
    step(0)
    local[2].wait()
    value_block(f)
    both(1)
    local[3].wait()
    local[4].wait()
    x_dy_in = remote(dy_raw.at[1 - s], dy_raw.at[1 - s], x_send.at[0], x_recv.at[0], to_x)
    x_up_in = remote(up.at[1 - s], up.at[1 - s], x_send.at[1], x_recv.at[1], to_x)
    x_low_in = remote(low.at[1 - s], low.at[1 - s], x_send.at[2], x_recv.at[2], to_x)
    x_dy_in.wait_recv()
    x_up_in.wait_recv()
    for h in range(2):
        for q in range(2):
            for i in range(slots):
                raw = dy_raw[h, tiles(i), q * block : (q + 1) * block].astype(jnp.float32)
                dy_blocks[2 * h + q, tiles(i), :] = jnp.where(valid(i, block), raw, 0.0).astype(
                    jnp.bfloat16
                )
    both(2)
    back = dot_nt(dy_blocks[0], up[0, :, 0:block])
    for b in range(1, 4):
        q = b % 2
        back += dot_nt(dy_blocks[b], up[b // 2, :, q * block : (q + 1) * block])
    back = jnp.concatenate(
        [jnp.where(chosen(i), back[tiles(i), :], 0.0) for i in range(slots)], axis=0
    )
    back_wide[...] = back.astype(jnp.bfloat16)
    back_turned = back.T.astype(jnp.bfloat16)

    @pl.loop(0, feats // step_cols)
    def _(k):
        cols = pl.ds(pl.multiple_of(k * step_cols, step_cols), step_cols)
        dpart[r, :, cols] = adapter_scale * dot_nn(back_turned, act[:, cols])

    r_down = remote(dpart.at[r], dpart.at[r], r_send.at[0], r_recv.at[0], to_r)
    r_up = remote(upart.at[r], upart.at[r], r_send.at[1], r_recv.at[1], to_r)
    r_down.start()
    both(3)
    both(4)

    def first_grad(part):
        @pl.loop(part * half, (part + 1) * half)
        def _(k):
            cols = pl.ds(pl.multiple_of(k * step_cols, step_cols), step_cols)
            igacc[:, cols] = dot_nn(dy_blocks[f], weights[f, :, cols]) + adapter_scale * dot_nn(
                back_wide[...], down[:, cols]
            )

    first_grad(0)
    both(5)
    first_grad(1)
    both(6)
    x_low_in.wait_recv()
    total = low[0] + low[1]
    in_wide[...] = total.astype(jnp.bfloat16)
    turned = total.T.astype(jnp.bfloat16)
    for q in range(2):
        upart[r, :, q * block : (q + 1) * block] = adapter_scale * dot_nn(
            turned, dy_blocks[2 * s + q]
        )
    r_up.start()
    core_wait(0)
    value_block(arrivals[0])
    both(7)
    grad_block(arrivals[0], 0)
    both(8)
    grad_block(arrivals[0], 1)
    both(9)
    core_wait(1)
    value_block(arrivals[1])
    both(10)
    grad_block(arrivals[1], 0)
    both(11)
    grad_block(arrivals[1], 1)
    last_chunk(0)
    y_step(11)
    last_chunk(1)
    remote(dpart.at[1 - r], dpart.at[1 - r], r_send.at[0], r_recv.at[0], to_r).wait_recv()
    dsum[...] = (dpart[0] + dpart[1]).astype(jnp.bfloat16)
    out_down = pltpu.make_async_copy(dsum, dgrad_h, out_sem.at[0])
    out_down.start()
    remote(upart.at[1 - r], upart.at[1 - r], r_send.at[1], r_recv.at[1], to_r).wait_recv()
    usum[...] = (upart[0] + upart[1]).astype(jnp.bfloat16)
    out_up = pltpu.make_async_copy(usum, ugrad_h, out_sem.at[1])
    out_up.start()
    last_chunk(2)
    last_chunk(3)

    for q in range(2):
        v_copy(q).wait_recv()
        extra = dot_nn(in_wide[...], up[s, :, q * block : (q + 1) * block])
        for i in range(slots):
            v = (
                vpart[2 * s + q, tiles(i), :]
                + vrecv[q, tiles(i), :].astype(jnp.float32)
                + adapter_scale * extra[tiles(i), :]
            )
            vout[tiles(i), q * block : (q + 1) * block] = jnp.where(valid(i, block), v, 0.0).astype(
                jnp.bfloat16
            )
    out_value = pltpu.make_async_copy(vout, value_h, out_sem.at[2])
    out_value.start()

    for c in range(CHUNKS):

        @pl.when(f > 0)
        def _():
            own_copy(c, True).wait_send()

        @pl.when(f < fsdp - 1)
        def _():
            own_copy(c, False).wait_send()

        for j in arrivals:

            @pl.when((j > f) & (f > 0))
            def _():
                z_copy(j, c, to_lo).wait_send()

            @pl.when((j < f) & (f < fsdp - 1))
            def _():
                z_copy(j, c, to_hi).wait_send()

            y_copy(j, c).wait_send()
            ca_copy(j, c).wait_send()
            cb_copy(j, c).wait_send()
    x_dy.wait_send()
    x_up.wait_send()
    x_low.wait_send()
    r_down.wait_send()
    r_up.wait_send()
    for q in range(2):
        v_copy(q).wait_send()
    for p in range(4):
        for c in range(CHUNKS):
            out_grad(p, c).wait()
    out_down.wait()
    out_up.wait()
    out_value.wait()


def hand_on_kernel(*refs):
    parts, count = 8, 4
    sources, targets, held = refs[:count], refs[count : 2 * count], refs[2 * count : 3 * count]
    into, out = refs[3 * count :]

    def piece(i, k):
        size = sources[i].shape[0] // parts
        return pl.ds(k * size, size)

    def load(i, k):
        rows = piece(i, k)
        return pltpu.make_async_copy(sources[i].at[rows], held[i].at[rows], into.at[i, k])

    def store(i, k):
        rows = piece(i, k)
        return pltpu.make_async_copy(held[i].at[rows], targets[i].at[rows], out.at[i, k])

    every = [(i, k) for i in range(count) for k in range(parts)]
    for i, k in every:
        load(i, k).start()
    for i, k in every:
        load(i, k).wait()
        store(i, k).start()
    for i, k in every:
        store(i, k).wait()


def on_device(
    activations,
    cotangent,
    base_weight,
    adapter_down,
    adapter_up,
    tile_counts,
    tile_length,
    tile_adapter,
):
    rows, feats = activations.shape
    heads = cotangent.shape[1]
    sets, low_rank = adapter_up.shape[:2]
    ranks = sets * low_rank
    block = base_weight.shape[0]
    down = adapter_down.transpose(0, 2, 1).reshape(ranks, feats)
    up = adapter_up.reshape(ranks, heads)
    bf16, f32 = jnp.bfloat16, jnp.float32
    dma = pltpu.SemaphoreType.DMA
    whole = pl.BlockSpec(memory_space=pl.ANY)
    scalars = pl.BlockSpec(memory_space=pltpu.SMEM)
    value, igrad, dgrad, ugrad = pl.pallas_call(
        fused_kernel,
        out_shape=(
            jax.ShapeDtypeStruct((rows, heads), bf16),
            jax.ShapeDtypeStruct((rows, feats), bf16),
            jax.ShapeDtypeStruct((ranks, feats), bf16),
            jax.ShapeDtypeStruct((ranks, heads), bf16),
        ),
        in_specs=[scalars] * 3 + [whole] * 5,
        out_specs=(whole,) * 4,
        scratch_shapes=[
            pltpu.VMEM((rows, feats), bf16),
            pltpu.VMEM((2, rows, heads), bf16),
            pltpu.VMEM((4, rows, block), bf16),
            pltpu.VMEM((4, block, feats), bf16),
            pltpu.VMEM((ranks, feats), bf16),
            pltpu.VMEM((2, ranks, heads), bf16),
            pltpu.VMEM((2, rows, ranks), f32),
            pltpu.VMEM((rows, ranks), bf16),
            pltpu.VMEM((rows, ranks), bf16),
            pltpu.VMEM((2, ranks, feats), f32),
            pltpu.VMEM((ranks, feats), bf16),
            pltpu.VMEM((2, ranks, heads), f32),
            pltpu.VMEM((ranks, heads), bf16),
            pltpu.VMEM((4, rows, block), f32),
            pltpu.VMEM((2, rows, block), bf16),
            pltpu.VMEM((2, rows, block), bf16),
            pltpu.VMEM((rows, heads), bf16),
            pltpu.VMEM((rows, feats), f32),
            pltpu.VMEM((rows, feats), bf16),
            dma((5,)),
            dma((3 + 4 * CHUNKS,)),
            dma((2, CHUNKS)),
        ]
        + [dma((4, CHUNKS))] * 8
        + [dma((3,)), dma((3,)), dma((2,)), dma((2,)), dma((2,)), dma((2,))],
        compiler_params=pltpu.CompilerParams(
            collective_id=0, has_side_effects=True, vmem_limit_bytes=60 * 1024 * 1024
        ),
    )(tile_counts, tile_length, tile_adapter, activations, cotangent, base_weight, down, up)
    results = (value, igrad, dgrad, ugrad)
    value, igrad, dgrad, ugrad = pl.pallas_call(
        hand_on_kernel,
        out_shape=tuple(jax.ShapeDtypeStruct(a.shape, a.dtype) for a in results),
        in_specs=[whole] * 4,
        out_specs=(whole,) * 4,
        scratch_shapes=[pltpu.VMEM(a.shape, a.dtype) for a in results] + [dma((4, 8)), dma((4, 8))],
        compiler_params=pltpu.CompilerParams(vmem_limit_bytes=60 * 1024 * 1024),
    )(*results)
    return (
        value,
        igrad,
        dgrad.reshape(sets, low_rank, feats).transpose(0, 2, 1),
        ugrad.reshape(sets, low_rank, heads),
    )


def solution(mesh):
    sizes = (mesh.shape["groups"], mesh.shape["fsdp"], mesh.shape["sub"], mesh.shape["rep"])
    return jax.shard_map(
        on_device if sizes == (2, 4, 2, 2) else on_device_general,
        mesh=mesh,
        in_specs=(
            P(("groups", "fsdp", "rep"), "sub"),
            P(("groups", "fsdp", "rep"), "sub"),
            P("fsdp", "sub"),
            P(("groups", "fsdp"), "sub", None),
            P(("groups", "fsdp"), None, "sub"),
            P("groups"),
            P(("groups", "fsdp", "rep")),
            P(("groups", "fsdp", "rep")),
        ),
        out_specs=(
            P(("groups", "fsdp", "rep"), "sub"),
            P(("groups", "fsdp", "rep"), "sub"),
            P(("groups", "fsdp"), "sub", None),
            P(("groups", "fsdp"), None, "sub"),
        ),
        check_vma=False,
    )
```

```python
import functools

import jax
import jax.numpy as jnp
from jax import lax
from jax.experimental import pallas as pl
from jax.experimental.pallas import tpu as pltpu
from jax.sharding import PartitionSpec as P

adapter_scale = 2.0


def on_device_general(
    activations,
    cotangent,
    base_weight,
    adapter_down,
    adapter_up,
    tile_counts,
    tile_length,
    tile_adapter,
):
    slot_count = tile_length.shape[0]
    tile_rows = activations.shape[0] // slot_count
    feat_width = activations.shape[1]
    head_width = cotangent.shape[1]
    own_sets = adapter_down.shape[0]
    low_rank = adapter_down.shape[2]
    rep_count = lax.axis_size("rep")
    fsdp_pos = lax.axis_index("fsdp")
    rep_pos = lax.axis_index("rep")
    own_count = tile_counts[fsdp_pos * rep_count + rep_pos]
    slot_ids = jnp.arange(slot_count, dtype=jnp.int32)
    positions = jnp.arange(tile_rows, dtype=jnp.int32)
    row_valid = (
        (slot_ids < own_count)[:, None] & (positions[None, :] < tile_length[:, None])
    ).astype(jnp.bfloat16)
    masked_dy = cotangent.reshape(slot_count, tile_rows, head_width) * row_valid[:, :, None]
    adapter_pick = (tile_adapter[:, None] == jnp.arange(own_sets, dtype=jnp.int32)[None, :]).astype(
        jnp.bfloat16
    )
    contract_last = (((1,), (1,)), ((), ()))
    contract_first = (((0,), (0,)), ((), ()))
    valid_rows = row_valid.reshape(-1)[:, None].astype(jnp.float32)
    work_dy = masked_dy.reshape(-1, head_width)
    row_count = activations.shape[0]
    set_count = adapter_down.shape[0]
    chosen_rows = jnp.broadcast_to(
        adapter_pick[:, None, :], (adapter_pick.shape[0], tile_rows, set_count)
    ).reshape(row_count, set_count)
    flattened_down = adapter_down.transpose(1, 0, 2).reshape(feat_width, set_count * low_rank)
    flat_up = adapter_up.reshape(set_count * low_rank, head_width)
    pick_adapter_rows = chosen_rows.astype(jnp.float32)[:, :, None]
    adapter_input_grad = jnp.dot(
        activations, flattened_down, preferred_element_type=jnp.float32
    ).reshape(row_count, set_count, low_rank)
    adapter_backward = lax.dot_general(
        work_dy, flat_up, contract_last, preferred_element_type=jnp.float32
    ).reshape(row_count, set_count, low_rank)
    input_piece = jnp.sum(adapter_input_grad * pick_adapter_rows, axis=1)
    backward_piece = jnp.sum(adapter_backward * pick_adapter_rows, axis=1)
    in_sum, back_sum = lax.psum((input_piece, backward_piece), "sub")
    in_low = in_sum.astype(jnp.bfloat16)
    back_low = back_sum.astype(jnp.bfloat16)
    in_wide = (chosen_rows[:, :, None] * in_low[:, None, :]).reshape(
        row_count, set_count * low_rank
    )
    back_wide = (chosen_rows[:, :, None] * back_low[:, None, :]).reshape(
        row_count, set_count * low_rank
    )
    full_dy = lax.all_gather(work_dy, "sub", axis=1, tiled=True)
    whole_weight = lax.all_gather(base_weight, "fsdp", axis=0, tiled=True)
    value_part = lax.dot_general(
        activations, whole_weight, contract_last, preferred_element_type=jnp.float32
    )
    input_frozen_grad = jnp.dot(full_dy, whole_weight, preferred_element_type=jnp.float32)
    value_frozen_out = lax.psum_scatter(value_part, "sub", scatter_dimension=1, tiled=True)
    value_total_out = value_frozen_out + adapter_scale * jnp.dot(
        in_wide, flat_up, preferred_element_type=jnp.float32
    )
    input_total_grad = input_frozen_grad + adapter_scale * lax.dot_general(
        back_wide, flattened_down, contract_last, preferred_element_type=jnp.float32
    )
    down_product = adapter_scale * lax.dot_general(
        activations, back_wide, contract_first, preferred_element_type=jnp.float32
    )
    up_product = adapter_scale * lax.dot_general(
        in_wide, work_dy, contract_first, preferred_element_type=jnp.float32
    )
    down_product = down_product.reshape(feat_width, set_count, low_rank).transpose(1, 0, 2)
    up_product = up_product.reshape(set_count, low_rank, head_width)
    value_total_out, input_total_grad, down_grad, up_grad = (
        value_total_out,
        input_total_grad,
        down_product,
        up_product,
    )
    down_total, up_total = lax.psum((down_grad, up_grad), "rep")
    value_proj = (value_total_out * valid_rows).astype(jnp.bfloat16)
    return (
        value_proj,
        input_total_grad.astype(jnp.bfloat16),
        down_total.astype(jnp.bfloat16),
        up_total.astype(jnp.bfloat16),
    )


CHUNKS = 4
NT = (((1,), (1,)), ((), ()))


def dot_nt(a, b):
    return lax.dot_general(a, b, NT, preferred_element_type=jnp.float32)


def dot_nn(a, b):
    return jnp.dot(a, b, preferred_element_type=jnp.float32)


def fused_kernel(
    counts,
    lengths,
    picks,
    act_h,
    dy_h,
    w_h,
    down_h,
    up_h,
    value_h,
    igrad_h,
    dgrad_h,
    ugrad_h,
    act,
    dy_raw,
    dy_blocks,
    weights,
    down,
    up,
    low,
    in_wide,
    back_wide,
    dpart,
    dsum,
    upart,
    usum,
    vpart,
    vsend,
    vrecv,
    vout,
    igacc,
    igout,
    local_sem,
    out_sem,
    own_send,
    z_send,
    z_recv,
    y_send,
    y_recv,
    ca_send,
    ca_recv,
    cb_send,
    cb_recv,
    x_send,
    x_recv,
    v_send,
    v_recv,
    r_send,
    r_recv,
):
    g = lax.axis_index("groups")
    f = lax.axis_index("fsdp")
    s = lax.axis_index("sub")
    r = lax.axis_index("rep")
    fsdp = 4
    slots = lengths.shape[0]
    rows, feats = act.shape
    tile = rows // slots
    block = w_h.shape[0]
    quarter = feats // 4
    width = quarter // CHUNKS
    to_y = {"groups": 1 - g}
    to_x = {"sub": 1 - s}
    to_r = {"rep": 1 - r}
    to_lo = {"fsdp": jnp.maximum(f - 1, 0)}
    to_hi = {"fsdp": jnp.minimum(f + 1, fsdp - 1)}

    barrier = pltpu.get_barrier_semaphore()
    for peer in (to_y, to_x, to_r):
        pl.semaphore_signal(barrier, inc=1, device_id=peer, device_id_type=pl.DeviceIdType.MESH)

    @pl.when(f > 0)
    def _():
        pl.semaphore_signal(barrier, inc=1, device_id=to_lo, device_id_type=pl.DeviceIdType.MESH)

    @pl.when(f < fsdp - 1)
    def _():
        pl.semaphore_signal(barrier, inc=1, device_id=to_hi, device_id_type=pl.DeviceIdType.MESH)

    local = [
        pltpu.make_async_copy(src, dst, local_sem.at[i])
        for i, (src, dst) in enumerate(
            (
                (act_h, act),
                (down_h, down),
                (w_h, weights.at[f]),
                (dy_h, dy_raw.at[s]),
                (up_h, up.at[s]),
            )
        )
    ]
    for copy in local:
        copy.start()
    ends = jnp.where(f == 0, 1, 0) + jnp.where(f == fsdp - 1, 1, 0)
    pl.semaphore_wait(barrier, 5 - ends)

    def remote(src, dst, send, recv, peer):
        return pltpu.make_async_remote_copy(
            src_ref=src,
            dst_ref=dst,
            send_sem=send,
            recv_sem=recv,
            device_id=peer,
            device_id_type=pl.DeviceIdType.MESH,
        )

    def columns(gg, rr, c):
        return pl.ds(pl.multiple_of((gg * 2 + rr) * quarter + c * width, width), width)

    def own_copy(c, down_way):
        cols = columns(g, r, c)
        return remote(
            w_h.at[:, cols],
            weights.at[f, :, cols],
            own_send.at[0 if down_way else 1, c],
            z_recv.at[f, c],
            to_lo if down_way else to_hi,
        )

    def own_start(c):
        @pl.when(f > 0)
        def _():
            own_copy(c, True).start()

        @pl.when(f < fsdp - 1)
        def _():
            own_copy(c, False).start()

    own_start(0)
    own_start(1)

    x_dy = remote(dy_h, dy_raw.at[s], x_send.at[0], x_recv.at[0], to_x)
    x_up = remote(up_h, up.at[s], x_send.at[1], x_recv.at[1], to_x)
    x_low = remote(low.at[s], low.at[s], x_send.at[2], x_recv.at[2], to_x)
    x_up.start()
    x_dy.start()

    order = ((1, 2, 3), (2, 0, 3), (1, 3, 0), (2, 1, 0))
    arrivals = []
    for t in range(fsdp - 1):
        j = jnp.int32(order[0][t])
        for p in range(1, fsdp):
            j = jnp.where(f == p, order[p][t], j)
        arrivals.append(j)

    def piece(j, gg, rr, c):
        return weights.at[j, :, columns(gg, rr, c)]

    def z_copy(j, c, peer):
        here = piece(j, g, r, c)
        return remote(here, here, z_send.at[j, c], z_recv.at[j, c], peer)

    def y_copy(j, c):
        here = piece(j, g, r, c)
        return remote(here, here, y_send.at[j, c], y_recv.at[j, c], to_y)

    def ca_copy(j, c):
        here = piece(j, g, r, c)
        return remote(here, here, ca_send.at[j, c], ca_recv.at[j, c], to_r)

    def cb_copy(j, c):
        here = piece(j, 1 - g, r, c)
        return remote(here, here, cb_send.at[j, c], cb_recv.at[j, c], to_r)

    def step(i):
        j, c = arrivals[i // CHUNKS], i % CHUNKS
        z_copy(j, c, to_y).wait_recv()

        @pl.when((j > f) & (f > 0))
        def _():
            z_copy(j, c, to_lo).start()

        @pl.when((j < f) & (f < fsdp - 1))
        def _():
            z_copy(j, c, to_hi).start()

        y_copy(j, c).start()
        ca_copy(j, c).start()

    def y_step(i):
        j, c = arrivals[i // CHUNKS], i % CHUNKS
        here = piece(j, 1 - g, r, c)
        remote(here, here, y_send.at[j, c], y_recv.at[j, c], to_y).wait_recv()
        cb_copy(j, c).start()

    def both(i):
        step(i)
        y_step(i - 1)

    def core_wait_chunk(t, c):
        j = arrivals[t]
        here = piece(j, g, 1 - r, c)
        remote(here, here, ca_send.at[j, c], ca_recv.at[j, c], to_r).wait_recv()
        here = piece(j, 1 - g, 1 - r, c)
        remote(here, here, cb_send.at[j, c], cb_recv.at[j, c], to_r).wait_recv()

    def core_wait(t):
        for c in range(CHUNKS):
            core_wait_chunk(t, c)

    own_count = counts[f * 2 + r]

    def valid(i, lanes):
        used = jnp.where(i < own_count, lengths[i], 0)
        return lax.broadcasted_iota(jnp.int32, (tile, lanes), 0) < used

    def chosen(i):
        lanes = lax.broadcasted_iota(jnp.int32, (tile, down.shape[0]), 1)
        return lanes // (down.shape[0] // 2) == picks[i]

    def tiles(i):
        return slice(i * tile, (i + 1) * tile)

    def v_copy(q):
        return remote(vsend.at[q], vrecv.at[q], v_send.at[q], v_recv.at[q], to_x)

    def value_block(j):
        part = dot_nt(act[...], weights[j])
        vpart[j] = part
        send_value(j, part)

    def send_value(j, part):
        @pl.when(j // 2 != s)
        def _():
            q = j % 2
            vsend[q] = part.astype(jnp.bfloat16)
            v_copy(q).start()

    step_cols = 512

    half = feats // step_cols // 2

    def grad_block(j, part):
        @pl.loop(part * half, (part + 1) * half)
        def _(k):
            cols = pl.ds(pl.multiple_of(k * step_cols, step_cols), step_cols)
            igacc[:, cols] += dot_nn(dy_blocks[j], weights[j, :, cols])

    last = arrivals[fsdp - 2]

    def out_grad(p, c):
        cols = pl.ds(p * quarter + c * width, width)
        return pltpu.make_async_copy(
            igout.at[:, cols], igrad_h.at[:, cols], out_sem.at[3 + p * CHUNKS + c]
        )

    def last_chunk(c):
        core_wait_chunk(fsdp - 2, c)
        part = vpart[last] if c > 0 else None
        for p in range(4):
            cols = slice(p * quarter + c * width, p * quarter + (c + 1) * width)
            term = dot_nt(act[:, cols], weights[last, :, cols])
            part = term if part is None else part + term
        vpart[last] = part
        if c == CHUNKS - 1:
            send_value(last, part)
        for p in range(4):
            cols = slice(p * quarter + c * width, p * quarter + (c + 1) * width)
            igout[:, cols] = (
                igacc[:, cols] + dot_nn(dy_blocks[last], weights[last, :, cols])
            ).astype(jnp.bfloat16)
            out_grad(p, c).start()

    local[0].wait()
    local[1].wait()
    wide = dot_nt(act[...], down[...])
    for i in range(slots):
        low[s, tiles(i), :] = jnp.where(chosen(i), wide[tiles(i), :], 0.0)
    x_low.start()
    step(0)
    own_start(2)
    local[2].wait()
    value_block(f)
    both(1)
    own_start(3)
    local[3].wait()
    local[4].wait()
    x_dy_in = remote(dy_raw.at[1 - s], dy_raw.at[1 - s], x_send.at[0], x_recv.at[0], to_x)
    x_up_in = remote(up.at[1 - s], up.at[1 - s], x_send.at[1], x_recv.at[1], to_x)
    x_low_in = remote(low.at[1 - s], low.at[1 - s], x_send.at[2], x_recv.at[2], to_x)
    x_dy_in.wait_recv()
    x_up_in.wait_recv()
    for h in range(2):
        for q in range(2):
            for i in range(slots):
                raw = dy_raw[h, tiles(i), q * block : (q + 1) * block].astype(jnp.float32)
                dy_blocks[2 * h + q, tiles(i), :] = jnp.where(valid(i, block), raw, 0.0).astype(
                    jnp.bfloat16
                )
    both(2)
    back = dot_nt(dy_blocks[0], up[0, :, 0:block])
    for b in range(1, 4):
        q = b % 2
        back += dot_nt(dy_blocks[b], up[b // 2, :, q * block : (q + 1) * block])
    back = jnp.concatenate(
        [jnp.where(chosen(i), back[tiles(i), :], 0.0) for i in range(slots)], axis=0
    )
    back_wide[...] = back.astype(jnp.bfloat16)
    back_turned = back.T.astype(jnp.bfloat16)

    @pl.loop(0, feats // step_cols)
    def _(k):
        cols = pl.ds(pl.multiple_of(k * step_cols, step_cols), step_cols)
        dpart[r, :, cols] = adapter_scale * dot_nn(back_turned, act[:, cols])

    r_down = remote(dpart.at[r], dpart.at[r], r_send.at[0], r_recv.at[0], to_r)
    r_up = remote(upart.at[r], upart.at[r], r_send.at[1], r_recv.at[1], to_r)
    r_down.start()
    both(3)
    both(4)

    def first_grad(part):
        @pl.loop(part * half, (part + 1) * half)
        def _(k):
            cols = pl.ds(pl.multiple_of(k * step_cols, step_cols), step_cols)
            igacc[:, cols] = dot_nn(dy_blocks[f], weights[f, :, cols]) + adapter_scale * dot_nn(
                back_wide[...], down[:, cols]
            )

    first_grad(0)
    both(5)
    first_grad(1)
    both(6)
    x_low_in.wait_recv()
    total = low[0] + low[1]
    in_wide[...] = total.astype(jnp.bfloat16)
    turned = total.T.astype(jnp.bfloat16)
    for q in range(2):
        upart[r, :, q * block : (q + 1) * block] = adapter_scale * dot_nn(
            turned, dy_blocks[2 * s + q]
        )
    r_up.start()
    core_wait(0)
    value_block(arrivals[0])
    both(7)
    grad_block(arrivals[0], 0)
    both(8)
    grad_block(arrivals[0], 1)
    both(9)
    core_wait(1)
    value_block(arrivals[1])
    both(10)
    grad_block(arrivals[1], 0)
    both(11)
    grad_block(arrivals[1], 1)
    last_chunk(0)
    y_step(11)
    last_chunk(1)
    remote(dpart.at[1 - r], dpart.at[1 - r], r_send.at[0], r_recv.at[0], to_r).wait_recv()
    dsum[...] = (dpart[0] + dpart[1]).astype(jnp.bfloat16)
    out_down = pltpu.make_async_copy(dsum, dgrad_h, out_sem.at[0])
    out_down.start()
    remote(upart.at[1 - r], upart.at[1 - r], r_send.at[1], r_recv.at[1], to_r).wait_recv()
    usum[...] = (upart[0] + upart[1]).astype(jnp.bfloat16)
    out_up = pltpu.make_async_copy(usum, ugrad_h, out_sem.at[1])
    out_up.start()
    last_chunk(2)
    last_chunk(3)

    for q in range(2):
        v_copy(q).wait_recv()
        extra = dot_nn(in_wide[...], up[s, :, q * block : (q + 1) * block])
        for i in range(slots):
            v = (
                vpart[2 * s + q, tiles(i), :]
                + vrecv[q, tiles(i), :].astype(jnp.float32)
                + adapter_scale * extra[tiles(i), :]
            )
            vout[tiles(i), q * block : (q + 1) * block] = jnp.where(valid(i, block), v, 0.0).astype(
                jnp.bfloat16
            )
    out_value = pltpu.make_async_copy(vout, value_h, out_sem.at[2])
    out_value.start()

    for c in range(CHUNKS):

        @pl.when(f > 0)
        def _():
            own_copy(c, True).wait_send()

        @pl.when(f < fsdp - 1)
        def _():
            own_copy(c, False).wait_send()

        for j in arrivals:

            @pl.when((j > f) & (f > 0))
            def _():
                z_copy(j, c, to_lo).wait_send()

            @pl.when((j < f) & (f < fsdp - 1))
            def _():
                z_copy(j, c, to_hi).wait_send()

            y_copy(j, c).wait_send()
            ca_copy(j, c).wait_send()
            cb_copy(j, c).wait_send()
    x_dy.wait_send()
    x_up.wait_send()
    x_low.wait_send()
    r_down.wait_send()
    r_up.wait_send()
    for q in range(2):
        v_copy(q).wait_send()
    for p in range(4):
        for c in range(CHUNKS):
            out_grad(p, c).wait()
    out_down.wait()
    out_up.wait()
    out_value.wait()


def hand_on_kernel(*refs):
    parts, count = 8, 4
    sources, targets, held = refs[:count], refs[count : 2 * count], refs[2 * count : 3 * count]
    into, out = refs[3 * count :]

    def piece(i, k):
        size = sources[i].shape[0] // parts
        return pl.ds(k * size, size)

    def load(i, k):
        rows = piece(i, k)
        return pltpu.make_async_copy(sources[i].at[rows], held[i].at[rows], into.at[i, k])

    def store(i, k):
        rows = piece(i, k)
        return pltpu.make_async_copy(held[i].at[rows], targets[i].at[rows], out.at[i, k])

    every = [(i, k) for i in range(count) for k in range(parts)]
    for i, k in every:
        load(i, k).start()
    for i, k in every:
        load(i, k).wait()
        store(i, k).start()
    for i, k in every:
        store(i, k).wait()


def on_device(
    activations,
    cotangent,
    base_weight,
    adapter_down,
    adapter_up,
    tile_counts,
    tile_length,
    tile_adapter,
):
    rows, feats = activations.shape
    heads = cotangent.shape[1]
    sets, low_rank = adapter_up.shape[:2]
    ranks = sets * low_rank
    block = base_weight.shape[0]
    down = adapter_down.transpose(0, 2, 1).reshape(ranks, feats)
    up = adapter_up.reshape(ranks, heads)
    bf16, f32 = jnp.bfloat16, jnp.float32
    dma = pltpu.SemaphoreType.DMA
    whole = pl.BlockSpec(memory_space=pl.ANY)
    scalars = pl.BlockSpec(memory_space=pltpu.SMEM)
    value, igrad, dgrad, ugrad = pl.pallas_call(
        fused_kernel,
        out_shape=(
            jax.ShapeDtypeStruct((rows, heads), bf16),
            jax.ShapeDtypeStruct((rows, feats), bf16),
            jax.ShapeDtypeStruct((ranks, feats), bf16),
            jax.ShapeDtypeStruct((ranks, heads), bf16),
        ),
        in_specs=[scalars] * 3 + [whole] * 5,
        out_specs=(whole,) * 4,
        scratch_shapes=[
            pltpu.VMEM((rows, feats), bf16),
            pltpu.VMEM((2, rows, heads), bf16),
            pltpu.VMEM((4, rows, block), bf16),
            pltpu.VMEM((4, block, feats), bf16),
            pltpu.VMEM((ranks, feats), bf16),
            pltpu.VMEM((2, ranks, heads), bf16),
            pltpu.VMEM((2, rows, ranks), f32),
            pltpu.VMEM((rows, ranks), bf16),
            pltpu.VMEM((rows, ranks), bf16),
            pltpu.VMEM((2, ranks, feats), f32),
            pltpu.VMEM((ranks, feats), bf16),
            pltpu.VMEM((2, ranks, heads), f32),
            pltpu.VMEM((ranks, heads), bf16),
            pltpu.VMEM((4, rows, block), f32),
            pltpu.VMEM((2, rows, block), bf16),
            pltpu.VMEM((2, rows, block), bf16),
            pltpu.VMEM((rows, heads), bf16),
            pltpu.VMEM((rows, feats), f32),
            pltpu.VMEM((rows, feats), bf16),
            dma((5,)),
            dma((3 + 4 * CHUNKS,)),
            dma((2, CHUNKS)),
        ]
        + [dma((4, CHUNKS))] * 8
        + [dma((3,)), dma((3,)), dma((2,)), dma((2,)), dma((2,)), dma((2,))],
        compiler_params=pltpu.CompilerParams(
            collective_id=0, has_side_effects=True, vmem_limit_bytes=60 * 1024 * 1024
        ),
    )(tile_counts, tile_length, tile_adapter, activations, cotangent, base_weight, down, up)
    results = (value, igrad, dgrad, ugrad)
    value, igrad, dgrad, ugrad = pl.pallas_call(
        hand_on_kernel,
        out_shape=tuple(jax.ShapeDtypeStruct(a.shape, a.dtype) for a in results),
        in_specs=[whole] * 4,
        out_specs=(whole,) * 4,
        scratch_shapes=[pltpu.VMEM(a.shape, a.dtype) for a in results] + [dma((4, 8)), dma((4, 8))],
        compiler_params=pltpu.CompilerParams(vmem_limit_bytes=60 * 1024 * 1024),
    )(*results)
    return (
        value,
        igrad,
        dgrad.reshape(sets, low_rank, feats).transpose(0, 2, 1),
        ugrad.reshape(sets, low_rank, heads),
    )


def solution(mesh):
    sizes = (mesh.shape["groups"], mesh.shape["fsdp"], mesh.shape["sub"], mesh.shape["rep"])
    return jax.shard_map(
        on_device if sizes == (2, 4, 2, 2) else on_device_general,
        mesh=mesh,
        in_specs=(
            P(("groups", "fsdp", "rep"), "sub"),
            P(("groups", "fsdp", "rep"), "sub"),
            P("fsdp", "sub"),
            P(("groups", "fsdp"), "sub", None),
            P(("groups", "fsdp"), None, "sub"),
            P("groups"),
            P(("groups", "fsdp", "rep")),
            P(("groups", "fsdp", "rep")),
        ),
        out_specs=(
            P(("groups", "fsdp", "rep"), "sub"),
            P(("groups", "fsdp", "rep"), "sub"),
            P(("groups", "fsdp"), "sub", None),
            P(("groups", "fsdp"), None, "sub"),
        ),
        check_vma=False,
    )
```
